32 devices in a mesh: wide: 16 (over z, y, x), deep: 2 (over core).
Axes of the slice: x: 2, y: 2, z: 4, core: 2. Of those that a mesh axis runs over, the one named last changes fastest.
Arguments:
- rhs_local: float32 [256, 32, 128], P('wide', 'deep'), may hold values from -6 to 6
- metric: float32 [3, 256, 32, 128], P(None, 'wide', 'deep'), may hold values from 0.005 to 0.05
- helm: float32 [256, 32, 128], P('wide', 'deep'), may hold values from 0.5 to 4
- columns: int32 [16, 4, 4, 8], P('wide', 'deep'), may hold values from 0 to 23
- live_blocks: int32 [16, 4, 4], P('wide', 'deep'), may hold values from 1 to 8
- block_values: float32 [16, 4, 4, 512], P('wide', 'deep'), may hold values from -0.0234375 to 0.0234375
Outputs:
- smoothed: float32 [256, 32, 128], P('wide', 'deep')
- coarse_product: float32 [16, 4, 32], P('wide', 'deep')
The draws below stay inside these ranges and needn't reach their ends.
All inputs are finite; a program needn't handle non-finite values.
Results may differ from the reference program's by a relative error of at most 0.00013.
Values sent between devices are 32-bit elements; how exact they have to be, the bound alone decides.
A program may use at most 64 MiB of HBM per device.

```python
import math
import jax
import jax.numpy as jnp
import numpy as np
from jax import lax

NP = 8
EY = 2
ZL = 1
DEGREE = 2
K = 8
BS = 8
EZ = 16
NXV = 32
NYV = 4
NXB = 4
NBL = 8
NX = 256
NY = 32
NZ = 128
N_WIDE = 16
N_DEEP = 2


def draw_live_blocks(key, part):
    counts = jax.random.randint(key, (EZ, NYV, NXB), 1, K + 1)
    return counts.at[0, 0, 0].set(K).astype(jnp.int32)


def plant(entries, own_key, least, top_value):
    dims = entries.shape
    place = [jax.random.randint(jax.random.fold_in(own_key, axis), (), 0, dims[axis]) for axis in range(len(dims))]
    entries = entries.at[tuple(place)].set(least)
    longest = dims.index(max(dims))
    place[longest] = (place[longest] + 1) % dims[longest]
    return entries.at[tuple(place)].set(top_value)


def steps_of(key, shape, cuts, least, largest):
    loudness = 1.0
    for dim, shards_of in cuts:
        steps = jax.random.uniform(jax.random.fold_in(jax.random.fold_in(key, 6), dim), (shards_of,), jnp.float32, least / len(cuts), largest / len(cuts))
        loudness = loudness * jnp.repeat(jnp.exp(steps), shape[dim] // shards_of).reshape((-1,) + (1,) * (len(shape) - 1 - dim))
    return loudness


def scatter_about(stream_key, shape, deviation, limit, shards=(), kind=jnp.bfloat16):
    drawn = jax.random.normal(stream_key, shape, jnp.float32) * deviation
    if len(shards) > 0:
        drawn = steps_of(stream_key, shape, shards, -0.22, 0.18) * drawn
    return jnp.clip(drawn, min=-limit, max=limit).astype(kind)


def setup_inputs(seed: int = 0) -> dict:
    arg_keys = jax.random.split(jax.random.key(seed), 7)
    return {
        "rhs_local": scatter_about(arg_keys[0], (NX, NY, NZ), 1.0, 6.0, ((0, 16), (1, 2)), jnp.float32),
        "metric": jnp.clip(jnp.exp(math.log(0.05) - 2.3025851 * jax.random.uniform(arg_keys[1], (3, NX, NY, NZ), jnp.float32) ** steps_of(arg_keys[1], (3, NX, NY, NZ), ((1, 16), (2, 2)), -0.2, 0.2)), 0.005, 0.05),
        "helm": jnp.clip(jnp.exp(math.log(4.0) - 2.0794415 * jax.random.uniform(arg_keys[2], (NX, NY, NZ), jnp.float32) ** steps_of(arg_keys[2], (NX, NY, NZ), ((0, 16), (1, 2)), -0.2, 0.2)), 0.5, 4.0),
        "columns": plant(jax.random.randint(arg_keys[3], (EZ, NYV, NXB, K), 0, 3 * NBL), jax.random.fold_in(arg_keys[3], 1), 0, (3 * NBL) - 1).astype(jnp.int32),
        "live_blocks": draw_live_blocks(jax.random.fold_in(arg_keys[6], 71), 0),
        "block_values": scatter_about(arg_keys[5], (EZ, NYV, NXB, K * BS * BS), (2 * K * BS * NP**3) ** -0.5, 0.0234375, ((0, 16), (1, 2)), jnp.float32),
    }


upper_bound = 6.0
lower_bound = 0.6
highest = lax.Precision.HIGHEST
forward_forms = ("mi,aibjck->ambjck", "mj,aibjck->aibmck", "mk,aibjck->aibjcm")
backward_forms = ("mi,ambjck->aibjck", "mj,aibmck->aibjck", "mk,aibjcm->aibjck")


def gll_tables(count):
    order = count - 1
    nodes = np.cos(np.pi * np.arange(count) / order)
    legendre = np.zeros((count, count))
    for sweep in range(101):
        legendre[:, 0] = 1.0
        legendre[:, 1] = nodes
        for degree in range(2, count):
            legendre[:, degree] = ((2 * degree - 1) * nodes * legendre[:, degree - 1] - (degree - 1) * legendre[:, degree - 2]) / degree
        if sweep < 100:
            nodes = nodes - (nodes * legendre[:, order] - legendre[:, order - 1]) / (count * legendre[:, order])
    nodes = nodes[::-1].copy()
    values = legendre[::-1, order].copy()
    identity_table = np.eye(count)
    spacing = nodes[:, None] - nodes[None, :] + identity_table
    derivative = values[:, None] / values[None, :] / spacing
    derivative = derivative * (1.0 - identity_table)
    derivative[0, 0] = -order * (order + 1) / 4.0
    derivative[-1, -1] = order * (order + 1) / 4.0
    linear = np.stack([(1.0 - nodes) / 2.0, (1.0 + nodes) / 2.0], axis=1)
    return jnp.asarray(derivative, jnp.float32), jnp.asarray(linear, jnp.float32)


def as_elements(field, count):
    shape = field.shape
    return field.reshape(shape[0] // count, count, shape[1] // count, count, shape[2] // count, count)


def pair_sum(grid, axis, wrap):
    node_axis = 2 * axis + 1
    elem_axis = 2 * axis
    count = grid.shape[node_axis]
    first = lax.slice_in_dim(grid, 0, 1, axis=node_axis)
    inner = lax.slice_in_dim(grid, 1, count - 1, axis=node_axis)
    last = lax.slice_in_dim(grid, count - 1, count, axis=node_axis)
    if wrap:
        shared = last + jnp.roll(first, -1, axis=elem_axis)
        new_last = shared
        new_first = jnp.roll(shared, 1, axis=elem_axis)
    else:
        length = last.shape[elem_axis]
        shared = lax.slice_in_dim(last, 0, length - 1, axis=elem_axis) + lax.slice_in_dim(first, 1, length, axis=elem_axis)
        new_last = jnp.concatenate([shared, lax.slice_in_dim(last, length - 1, length, axis=elem_axis)], axis=elem_axis)
        new_first = jnp.concatenate([lax.slice_in_dim(first, 0, 1, axis=elem_axis), shared], axis=elem_axis)
    return jnp.concatenate([new_first, inner, new_last], axis=node_axis)


def assemble(field, count):
    grid = as_elements(field, count)
    for axis in range(3):
        grid = pair_sum(grid, axis, True)
    return grid.reshape(field.shape)


def apply_operator(field, metric, helm, derivative):
    count = derivative.shape[0]
    grid = as_elements(field, count)
    total = helm * field
    for axis in range(3):
        slope = jnp.einsum(forward_forms[axis], derivative, grid, precision=highest)
        flux = as_elements(metric[axis], count) * slope
        total = total + jnp.einsum(backward_forms[axis], derivative, flux, precision=highest).reshape(field.shape)
    return total


def operator_diagonal(metric, helm, derivative):
    count = derivative.shape[0]
    squares = derivative * derivative
    total = helm
    for axis in range(3):
        total = total + jnp.einsum(backward_forms[axis], squares, as_elements(metric[axis], count), precision=highest).reshape(helm.shape)
    return total


def chebyshev(solution, rhs_local, metric, helm, derivative, inverse, from_zero):
    centre = (upper_bound + lower_bound) / 2.0
    half_width = (upper_bound - lower_bound) / 2.0
    aspect = centre / half_width
    weight_prev = 1.0 / aspect
    if from_zero:
        residual = assemble(rhs_local, NP)
    else:
        residual = assemble(rhs_local - apply_operator(solution, metric, helm, derivative), NP)
    update = inverse * residual / centre
    solution = solution + update
    for turn in range(DEGREE - 1):
        residual = assemble(rhs_local - apply_operator(solution, metric, helm, derivative), NP)
        weight_next = 1.0 / (2.0 * aspect - weight_prev)
        update = weight_next * weight_prev * update + (2.0 * weight_next / half_width) * inverse * residual
        solution = solution + update
        weight_prev = weight_next
    return solution


def restrict(field, linear, count):
    grid = as_elements(field, count)
    small = jnp.einsum("ia,jb,kc,xiyjzk->xaybzc", linear, linear, linear, grid, precision=highest)
    shape = field.shape
    return small.reshape(shape[0] // count * 2, shape[1] // count * 2, shape[2] // count * 2)


def prolong_values(vertices, linear):
    shape = vertices.shape
    holder = jnp.zeros((shape[0], 2, shape[1], 2, shape[2], 2), jnp.float32)
    holder = holder.at[:, 0, :, 0, :, 0].set(vertices)
    summed = assemble(holder.reshape(shape[0] * 2, shape[1] * 2, shape[2] * 2), 2)
    grid = jnp.einsum("ia,jb,kc,xaybzc->xiyjzk", linear, linear, linear, as_elements(summed, 2), precision=highest)
    count = linear.shape[0]
    return grid.reshape(shape[0] * count, shape[1] * count, shape[2] * count)


def coarse_multiply(coarse_res, columns, live_blocks, block_values):
    owners = N_WIDE
    groups = N_DEEP
    per_owner = ZL * EY * NXB
    vectors = coarse_res.reshape(owners, ZL, groups, EY, NXB, BS).transpose(0, 2, 1, 3, 4, 5).reshape(owners, groups, per_owner, BS)
    frame = jnp.concatenate([jnp.roll(vectors, 1, axis=0), vectors, jnp.roll(vectors, -1, axis=0)], axis=2)
    frame_rows = frame.reshape(owners * groups * 3 * per_owner, BS)
    index = columns.reshape(owners, ZL, groups, EY, NXB, K).transpose(0, 2, 1, 3, 4, 5).reshape(owners, groups, per_owner * K)
    offsets = (jnp.arange(owners * groups, dtype=jnp.int32) * (3 * per_owner)).reshape(owners, groups, 1)
    picked = jnp.take(frame_rows, (index + offsets).reshape(-1), axis=0).reshape(owners, groups, per_owner, K, BS)
    counts = live_blocks.reshape(owners, ZL, groups, EY, NXB).transpose(0, 2, 1, 3, 4).reshape(owners, groups, per_owner)
    live = (jnp.arange(K, dtype=jnp.int32)[None, None, None, :] < counts[:, :, :, None]).astype(jnp.float32)
    values = block_values.reshape(owners, ZL, groups, EY, NXB, K, BS, BS).transpose(0, 2, 1, 3, 4, 5, 6, 7).reshape(owners, groups, per_owner, K, BS, BS)
    product = jnp.einsum("wdlkij,wdlkj,wdlk->wdli", values, picked, live, precision=highest)
    return product.reshape(owners, groups, ZL, EY, NXB, BS).transpose(0, 2, 1, 3, 4, 5).reshape(EZ, NYV, NXV)


def reference(rhs_local, metric, helm, columns, live_blocks, block_values):
    derivative, linear = gll_tables(NP)
    inverse = 1.0 / assemble(operator_diagonal(metric, helm, derivative), NP)
    first = chebyshev(jnp.zeros_like(rhs_local), rhs_local, metric, helm, derivative, inverse, True)
    local_res = rhs_local - apply_operator(first, metric, helm, derivative)
    assembled = assemble(restrict(local_res, linear, NP), 2)
    vertices = as_elements(assembled, 2)[:, 0, :, 0, :, 0]
    coarse_res = jnp.transpose(vertices, (2, 1, 0))
    coarse_product = coarse_multiply(coarse_res, columns, live_blocks, block_values)
    second = first + prolong_values(jnp.transpose(coarse_product, (2, 1, 0)), linear)
    smoothed = chebyshev(second, rhs_local, metric, helm, derivative, inverse, False)
    return smoothed, coarse_product
```

```python
import functools

import jax
import jax.numpy as jnp
import numpy as np
from jax import lax
from jax.experimental import pallas as pl
from jax.experimental.pallas import tpu as pltpu
from jax.sharding import PartitionSpec as P

NP = 8
K = 8
BS = 8
MESH = pl.DeviceIdType.MESH
F32 = jnp.float32
BF16 = jnp.bfloat16

upper_bound = 6.0
lower_bound = 0.6
centre = (upper_bound + lower_bound) / 2.0
half_width = (upper_bound - lower_bound) / 2.0
aspect = centre / half_width
first_weight = 1.0 / aspect
second_weight = 1.0 / (2.0 * aspect - first_weight)


def gll_tables(count):
    order = count - 1
    nodes = np.cos(np.pi * np.arange(count) / order)
    legendre = np.zeros((count, count))
    for sweep in range(101):
        legendre[:, 0] = 1.0
        legendre[:, 1] = nodes
        for degree in range(2, count):
            legendre[:, degree] = (
                (2 * degree - 1) * nodes * legendre[:, degree - 1]
                - (degree - 1) * legendre[:, degree - 2]
            ) / degree
        if sweep < 100:
            nodes = nodes - (nodes * legendre[:, order] - legendre[:, order - 1]) / (
                count * legendre[:, order]
            )
    nodes = nodes[::-1].copy()
    values = legendre[::-1, order].copy()
    identity_table = np.eye(count)
    spacing = nodes[:, None] - nodes[None, :] + identity_table
    derivative = values[:, None] / values[None, :] / spacing
    derivative = derivative * (1.0 - identity_table)
    derivative[0, 0] = -order * (order + 1) / 4.0
    derivative[-1, -1] = order * (order + 1) / 4.0
    linear = np.stack([(1.0 - nodes) / 2.0, (1.0 + nodes) / 2.0], axis=1)
    return derivative.astype(np.float32), linear.astype(np.float32)


def stacked_pieces(table):
    high = table.astype(jnp.bfloat16)
    low = (table - high.astype(np.float32)).astype(jnp.bfloat16)
    row = np.concatenate([high, low], axis=1)
    return np.concatenate([row, row], axis=0)


def tables_of(nw, nz):
    deriv, lin = gll_tables(NP)
    eye = np.eye(16, dtype=np.float32)
    square = deriv * deriv
    z_tables = np.stack(
        [
            stacked_pieces(np.kron(eye, deriv.T)),
            stacked_pieces(np.kron(eye, deriv)),
            stacked_pieces(np.kron(eye, square)),
        ]
    )
    node = np.arange(8)
    y_table = np.zeros((3, 8, 8, 128), np.float32)
    for shift in range(8):
        other = (node - shift) % 8
        y_table[0, shift] = deriv[node, other][:, None]
        y_table[1, shift] = deriv[other, node][:, None]
        y_table[2, shift] = square[other, node][:, None]
    three = np.zeros((3, 16), np.float32)
    three[0, :8] = lin[:, 0]
    three[1, :8] = lin[:, 1]
    three[1, 8:] = lin[:, 0]
    three[2, 8:] = lin[:, 1]
    corner = np.zeros((128, 256), np.float32)
    for layer in range(3):
        for yv in range(3):
            for xv in range(3):
                corner[layer * 16 + yv * 4 + xv] = np.kron(three[xv], three[yv])
    wz = np.zeros((nw, nz), np.float32)
    for v in range(nw):
        wz[v, v * 8 : v * 8 + 8] += lin[:, 0]
        back = (v - 1) % nw
        wz[v, back * 8 : back * 8 + 8] += lin[:, 1]
    wz3 = np.concatenate([np.roll(wz, 1, axis=0), wz, np.roll(wz, -1, axis=0)], axis=0)
    nb = 2 * (2 * nw // BS)
    rep = np.kron(np.eye(nb, dtype=np.float32), np.ones((1, 8), np.float32))
    pick = np.zeros((2 * nw, 8), np.float32)
    for par in range(2):
        for w in range(nw):
            pick[par * nw + w, 2 * (w % 4) + par] = 1.0
    return deriv, (
        jnp.asarray(z_tables),
        jnp.asarray(y_table),
        jnp.asarray(corner[:64]),
        jnp.asarray(wz3),
        jnp.asarray(rep),
        jnp.asarray(pick),
        jnp.asarray(np.ascontiguousarray(corner[:16].T)),
    )


def halves(value):
    high = value.astype(BF16)
    return high, (value - high.astype(F32)).astype(BF16)


def mm(a, b, transposed=False):
    dims = (((1,), (1 if transposed else 0,)), ((), ()))
    dot = functools.partial(lax.dot_general, dimension_numbers=dims, preferred_element_type=F32)
    ah, al = halves(a)
    bh, bl = halves(b)
    return dot(ah, bh) + (dot(al, bh) + dot(ah, bl))


def kernel(
    nw, nd, deriv,
    rhs_ref, metric_ref, helm_ref, columns_ref, live_ref, values_ref,
    zt_ref, yt_ref, corner_ref, wz3_ref, rep_ref, pick_ref, expand_ref,
    out_ref, product_ref,
    xs, ys, es, xr, yr, er, qs, qr, cs, cr, inv_ref, m_ref, spread_ref,
    face_send, face_recv, q_send, q_recv, c_send, c_recv,
):
    nz = rhs_ref.shape[2]
    nxb = 2 * nw // BS
    nb = 2 * nxb
    width = nb * 8
    w = lax.axis_index("wide")
    d = lax.axis_index("deep")
    left, right = lax.rem(w + nw - 1, nw), lax.rem(w + 1, nw)
    down, up = lax.rem(d + nd - 1, nd), lax.rem(d + 1, nd)
    around = [up] if nd == 2 else [down, up]

    barrier = pltpu.get_barrier_semaphore()

    def greet(step, carry):
        to = lax.rem(w + step, nw)
        for other in around:
            pl.semaphore_signal(
                barrier, inc=1, device_id={"wide": to, "deep": other}, device_id_type=MESH
            )

        @pl.when(step > 0)
        def _():
            pl.semaphore_signal(
                barrier, inc=1, device_id={"wide": to, "deep": d}, device_id_type=MESH
            )

        return carry

    lax.fori_loop(0, nw, greet, 0)

    rows = lax.broadcasted_iota(jnp.int32, (16, 8, nz), 1)
    lanes = lax.broadcasted_iota(jnp.int32, (16, 16, nz), 2) % 8
    plane = lax.broadcasted_iota(jnp.int32, (16, nz), 0)

    def local_sum(f):
        after = pltpu.roll(f.reshape(256, nz), nz - 1, 1).reshape(16, 16, nz)
        before = pltpu.roll(f.reshape(256, nz), 1, 1).reshape(16, 16, nz)
        f = f + jnp.where(lanes == 7, after, jnp.where(lanes == 0, before, 0.0))
        lo, hi = f[:, :8], f[:, 8:]
        new_lo = lo + jnp.where(rows == 7, pltpu.roll(hi, 7, 1), 0.0)
        new_hi = hi + jnp.where(rows == 0, pltpu.roll(lo, 1, 1), 0.0)
        f = jnp.concatenate([new_lo, new_hi], axis=1)
        shared = f[7:8] + f[8:9]
        return jnp.concatenate([f[:7], shared, shared, f[9:]], axis=0)

    def face_copies(turn):
        pairs = [
            (xs.at[turn, 1], xr.at[turn, 0], right, d),
            (xs.at[turn, 0], xr.at[turn, 1], left, d),
            (ys.at[turn, 1], yr.at[turn, 0], w, up),
            (ys.at[turn, 0], yr.at[turn, 1], w, down),
            (es.at[turn, 3], er.at[turn, 0], right, up),
            (es.at[turn, 2], er.at[turn, 1], right, down),
            (es.at[turn, 1], er.at[turn, 2], left, up),
            (es.at[turn, 0], er.at[turn, 3], left, down),
        ]
        return [
            pltpu.make_async_remote_copy(
                src_ref=src,
                dst_ref=dst,
                send_sem=face_send.at[turn, index],
                recv_sem=face_recv.at[turn, index],
                device_id={"wide": to_w, "deep": to_d},
                device_id_type=MESH,
            )
            for index, (src, dst, to_w, to_d) in enumerate(pairs)
        ]

    def begin(turn, f):
        f = local_sum(f)
        xs[turn, 0] = f[0]
        xs[turn, 1] = f[15]
        ys[turn, 0] = f[:, 0:1]
        ys[turn, 1] = f[:, 15:16]
        es[turn, 0] = f[0, 0:1]
        es[turn, 1] = f[0, 15:16]
        es[turn, 2] = f[15, 0:1]
        es[turn, 3] = f[15, 15:16]
        copies = face_copies(turn)
        for copy in copies:
            copy.start()
        return f, copies

    def finish(turn, f, copies):
        for copy in copies:
            copy.wait_recv()
        lo = f[:, :8] + jnp.where(rows == 0, yr[turn, 0], 0.0)
        hi = f[:, 8:] + jnp.where(rows == 7, yr[turn, 1], 0.0)
        f = jnp.concatenate([lo, hi], axis=1)

        def face(side):
            edge_lo, edge_hi = er[turn, 2 * side], er[turn, 2 * side + 1]
            return xr[turn, side] + jnp.where(
                plane == 0, edge_lo, jnp.where(plane == 15, edge_hi, 0.0)
            )

        return jnp.concatenate(
            [f[:1] + face(0)[None], f[1:15], f[15:] + face(1)[None]], axis=0
        )

    def x_apply(u, table):
        parts = u.reshape(2, 8, 16, nz)
        nodes = [parts[:, i] for i in range(8)]
        result = []
        for m in range(8):
            total = float(table[m, 0]) * nodes[0]
            for i in range(1, 8):
                total = total + float(table[m, i]) * nodes[i]
            result.append(total)
        return jnp.stack(result, axis=1).reshape(16, 16, nz)

    def y_apply(u, which):
        parts = u.reshape(32, 8, nz)

        def coefficient(shift):
            table = yt_ref[which, shift]
            if nz > 128:
                table = jnp.concatenate([table] * (nz // 128), axis=1)
            return table[None]

        total = coefficient(0) * parts
        for shift in range(1, 8):
            total = total + coefficient(shift) * pltpu.roll(parts, shift, 1)
        return total.reshape(16, 16, nz)

    def z_apply(u, which):
        flat = u.reshape(256, nz)
        result = []
        for start in range(0, nz, 128):
            high, low = halves(flat[:, start : start + 128])
            both = jnp.dot(
                jnp.concatenate([high, low], axis=1), zt_ref[which], preferred_element_type=F32
            )
            result.append(both[:, :128] + both[:, 128:])
        whole = result[0] if len(result) == 1 else jnp.concatenate(result, axis=1)
        return whole.reshape(16, 16, nz)

    def operator(u):
        total = helm_ref[...] * u
        total = total + x_apply(metric_ref[0] * x_apply(u, deriv), deriv.T)
        total = total + y_apply(metric_ref[1] * y_apply(u, 0), 1)
        return total + z_apply(metric_ref[2] * z_apply(u, 0), 1)

    square = deriv * deriv
    diagonal = helm_ref[...] + x_apply(metric_ref[0], square.T)
    diagonal = diagonal + y_apply(metric_ref[1], 2) + z_apply(metric_ref[2], 2)

    pl.semaphore_wait(barrier, nw * (1 + len(around)) - 1)
    diagonal, diagonal_copies = begin(0, diagonal)
    summed, rhs_copies = begin(1, rhs_ref[...])

    v = jnp.concatenate([values_ref[0, y] for y in range(2)], axis=0)
    spread = mm(v.T, rep_ref[...]).reshape(K, BS, BS, width)
    slot_lane = lax.broadcasted_iota(jnp.int32, (BS, width), 1) % 8
    cols = jnp.concatenate([columns_ref[0, y] for y in range(2)], axis=0).astype(F32)
    live = jnp.concatenate(
        [jnp.concatenate([live_ref[0, y : y + 1, b : b + 1] for b in range(nxb)], axis=0) for y in range(2)],
        axis=0,
    )
    slot = lax.broadcasted_iota(jnp.int32, (nb, K), 1)
    cols = jnp.where(slot < live, cols, -1.0)
    cols = jnp.dot(
        cols.T.astype(BF16), rep_ref[...].astype(BF16), preferred_element_type=F32
    ).astype(jnp.int32)
    block = lax.broadcasted_iota(jnp.int32, (nw, width), 0) // 4
    sums = [jnp.zeros((nw, width), F32) for _ in range(12)]
    for k in range(K):
        chosen = jnp.zeros((BS, width), F32)
        for i in range(BS):
            chosen = chosen + jnp.where(slot_lane == i, spread[k, i], 0.0)
        placed = mm(pick_ref[...], chosen)
        for layer in range(3):
            for y in range(2):
                hit = cols[k : k + 1] == block + (layer * nb + y * nxb)
                for par in range(2):
                    at = layer * 4 + y * 2 + par
                    sums[at] = sums[at] + jnp.where(
                        hit, placed[par * nw : (par + 1) * nw], 0.0
                    )
    for at in range(12):
        m_ref[at] = sums[at]

    vertex = lax.broadcasted_iota(jnp.int32, (16, 2 * width), 0)
    lane = lax.broadcasted_iota(jnp.int32, (16, 2 * width), 1)
    yv, xv = vertex // 4, vertex % 4
    wanted_x = lax.rem(2 * w + xv, 2 * nw)
    wanted = jnp.where(yv < 2, yv * 2 * nw, width) + wanted_x
    selected = jnp.where((lane == wanted) & (yv < 3) & (xv < 3), 1.0, 0.0)
    spread_ref[...] = mm(expand_ref[...], selected)

    inverse = 1.0 / finish(0, diagonal, diagonal_copies)
    inv_ref[...] = inverse
    residual = finish(1, summed, rhs_copies)
    update = inverse * residual * (1.0 / centre)
    u = update
    f, face_two = begin(2, rhs_ref[...] - operator(u))
    residual = finish(2, f, face_two)
    update = (second_weight * first_weight) * update + (
        (2.0 * second_weight / half_width) * inv_ref[...]
    ) * residual
    first = u + update

    local_res = rhs_ref[...] - operator(first)
    vertices = mm(corner_ref[...], local_res.reshape(256, nz))
    shifted = mm(wz3_ref[...], vertices, True)
    group = lax.broadcasted_iota(jnp.int32, (nw, 64), 1) // 16
    packed = jnp.where(
        group == 0,
        shifted[:nw],
        jnp.where(group == 1, shifted[nw : 2 * nw], shifted[2 * nw :]),
    )
    packed = jnp.concatenate([packed, jnp.zeros((nw, 64), F32)], axis=1)
    for row in range(nw):
        qs[row] = packed[row : row + 1]
    qr[0, w] = qs[w]

    def q_copy(to, to_d, which):
        return pltpu.make_async_remote_copy(
            src_ref=qs.at[to],
            dst_ref=qr.at[which, w],
            send_sem=q_send.at[which],
            recv_sem=q_recv.at[which],
            device_id={"wide": to, "deep": to_d},
            device_id_type=MESH,
        )

    def q_start(step, carry):
        to = lax.rem(w + step, nw)
        q_copy(to, up, 1).start()

        @pl.when(step > 0)
        def _():
            q_copy(to, d, 0).start()

        return carry

    lax.fori_loop(0, nw, q_start, 0)

    def wait_rows(ref, count, which, semaphore):
        view = ref.at[which, pl.ds(0, count)]
        pltpu.make_async_copy(view, view, semaphore).wait()

    wait_rows(qr, nw - 1, 0, q_recv.at[0])
    wait_rows(qr, nw, 1, q_recv.at[1])
    own = jnp.concatenate([qr[0, row] for row in range(nw)], axis=0)
    below = jnp.concatenate([qr[1, row] for row in range(nw)], axis=0)
    frame = own + pltpu.roll(below, 128 - 8, 1)
    frame = frame + pltpu.roll(pltpu.roll(frame, 1, 0), 128 - 2, 1)
    total = jnp.zeros((nw, width), F32)
    for layer in range(3):
        for y in range(2):
            for par in range(2):
                at = layer * 16 + y * 4 + par
                total = total + m_ref[layer * 4 + y * 2 + par] * frame[:, at : at + 1]
    product = jnp.sum(total, axis=0, keepdims=True)
    cs[0] = product
    cr[0, w] = product
    product_ref[0, 0:1] = product[:, : 2 * nw]
    product_ref[0, 1:2] = product[:, 2 * nw :]

    def c_copy(to, to_d, which):
        return pltpu.make_async_remote_copy(
            src_ref=cs.at[0],
            dst_ref=cr.at[which, w],
            send_sem=c_send.at[which],
            recv_sem=c_recv.at[which],
            device_id={"wide": to, "deep": to_d},
            device_id_type=MESH,
        )

    def c_start(step, carry):
        to = lax.rem(w + step, nw)
        c_copy(to, down, 1).start()

        @pl.when(step > 0)
        def _():
            c_copy(to, d, 0).start()

        return carry

    lax.fori_loop(0, nw, c_start, 0)
    wait_rows(cr, nw - 1, 0, c_recv.at[0])
    wait_rows(cr, nw, 1, c_recv.at[1])
    mine = jnp.concatenate([cr[0, row] for row in range(nw)], axis=0)
    above = jnp.concatenate([cr[1, row] for row in range(nw)], axis=0)
    both = jnp.concatenate([mine, above], axis=1)
    correction = mm(mm(spread_ref[...], both, True), wz3_ref[nw : 2 * nw])
    u = first + correction.reshape(16, 16, nz)

    f, face_three = begin(3, rhs_ref[...] - operator(u))
    update = inv_ref[...] * finish(3, f, face_three) * (1.0 / centre)
    u = u + update
    f, face_four = begin(4, rhs_ref[...] - operator(u))
    residual = finish(4, f, face_four)
    update = (second_weight * first_weight) * update + (
        (2.0 * second_weight / half_width) * inv_ref[...]
    ) * residual
    out_ref[...] = u + update

    for copies in (diagonal_copies, rhs_copies, face_two, face_three, face_four):
        for copy in copies:
            copy.wait_send()
    wait_rows(qr, nw - 1, 0, q_send.at[0])
    wait_rows(qr, nw, 1, q_send.at[1])
    wait_rows(cr, nw - 1, 0, c_send.at[0])
    wait_rows(cr, nw, 1, c_send.at[1])


def local(nw, nd, *arguments):
    rhs = arguments[0]
    nz = rhs.shape[2]
    deriv, tables = tables_of(nw, nz)
    width = 4 * nw
    vmem = pl.BlockSpec(memory_space=pltpu.VMEM)
    return pl.pallas_call(
        functools.partial(kernel, nw, nd, deriv),
        out_shape=(
            jax.ShapeDtypeStruct(rhs.shape, F32),
            jax.ShapeDtypeStruct((1, 2, 2 * nw), F32),
        ),
        in_specs=[vmem] * 13,
        out_specs=(vmem, vmem),
        scratch_shapes=[
            pltpu.VMEM((5, 2, 16, nz), F32),
            pltpu.VMEM((5, 2, 16, 1, nz), F32),
            pltpu.VMEM((5, 4, 1, nz), F32),
            pltpu.VMEM((5, 2, 16, nz), F32),
            pltpu.VMEM((5, 2, 16, 1, nz), F32),
            pltpu.VMEM((5, 4, 1, nz), F32),
            pltpu.VMEM((nw, 1, 128), F32),
            pltpu.VMEM((2, nw, 1, 128), F32),
            pltpu.VMEM((1, 1, width), F32),
            pltpu.VMEM((2, nw, 1, width), F32),
            pltpu.VMEM((16, 16, nz), F32),
            pltpu.VMEM((12, nw, width), F32),
            pltpu.VMEM((256, 2 * width), F32),
            pltpu.SemaphoreType.DMA((5, 8)),
            pltpu.SemaphoreType.DMA((5, 8)),
            pltpu.SemaphoreType.DMA((2,)),
            pltpu.SemaphoreType.DMA((2,)),
            pltpu.SemaphoreType.DMA((2,)),
            pltpu.SemaphoreType.DMA((2,)),
        ],
        compiler_params=pltpu.CompilerParams(
            collective_id=0, has_side_effects=True, vmem_limit_bytes=48 * 1024 * 1024
        ),
    )(*arguments, *tables)


def solution(mesh):
    placed = (
        P("wide", "deep", None),
        P(None, "wide", "deep", None),
        P("wide", "deep", None),
        P("wide", "deep", None, None),
        P("wide", "deep", None),
        P("wide", "deep", None, None),
    )
    return jax.shard_map(
        functools.partial(local, mesh.shape["wide"], mesh.shape["deep"]),
        mesh=mesh,
        in_specs=placed,
        out_specs=(P("wide", "deep", None), P("wide", "deep", None)),
        check_vma=False,
    )
```

```python
import functools

import jax
import jax.numpy as jnp
import numpy as np
from jax import lax
from jax.experimental import pallas as pl
from jax.experimental.pallas import tpu as pltpu
from jax.sharding import PartitionSpec as P

NP = 8
K = 8
BS = 8
MESH = pl.DeviceIdType.MESH
F32 = jnp.float32
BF16 = jnp.bfloat16

upper_bound = 6.0
lower_bound = 0.6
centre = (upper_bound + lower_bound) / 2.0
half_width = (upper_bound - lower_bound) / 2.0
aspect = centre / half_width
first_weight = 1.0 / aspect
second_weight = 1.0 / (2.0 * aspect - first_weight)


def gll_tables(count):
    order = count - 1
    nodes = np.cos(np.pi * np.arange(count) / order)
    legendre = np.zeros((count, count))
    for sweep in range(101):
        legendre[:, 0] = 1.0
        legendre[:, 1] = nodes
        for degree in range(2, count):
            legendre[:, degree] = (
                (2 * degree - 1) * nodes * legendre[:, degree - 1]
                - (degree - 1) * legendre[:, degree - 2]
            ) / degree
        if sweep < 100:
            nodes = nodes - (nodes * legendre[:, order] - legendre[:, order - 1]) / (
                count * legendre[:, order]
            )
    nodes = nodes[::-1].copy()
    values = legendre[::-1, order].copy()
    identity_table = np.eye(count)
    spacing = nodes[:, None] - nodes[None, :] + identity_table
    derivative = values[:, None] / values[None, :] / spacing
    derivative = derivative * (1.0 - identity_table)
    derivative[0, 0] = -order * (order + 1) / 4.0
    derivative[-1, -1] = order * (order + 1) / 4.0
    linear = np.stack([(1.0 - nodes) / 2.0, (1.0 + nodes) / 2.0], axis=1)
    return derivative.astype(np.float32), linear.astype(np.float32)


def stacked_pieces(table):
    high = table.astype(jnp.bfloat16)
    low = (table - high.astype(np.float32)).astype(jnp.bfloat16)
    row = np.concatenate([high, low], axis=1)
    return np.concatenate([row, row], axis=0)


def tables_of(nw, nz):
    deriv, lin = gll_tables(NP)
    eye = np.eye(16, dtype=np.float32)
    square = deriv * deriv
    z_tables = np.stack(
        [
            stacked_pieces(np.kron(eye, deriv.T)),
            stacked_pieces(np.kron(eye, deriv)),
            stacked_pieces(np.kron(eye, square)),
        ]
    )
    node = np.arange(8)
    y_table = np.zeros((3, 8, 8, 128), np.float32)
    for shift in range(8):
        other = (node - shift) % 8
        y_table[0, shift] = deriv[node, other][:, None]
        y_table[1, shift] = deriv[other, node][:, None]
        y_table[2, shift] = square[other, node][:, None]
    three = np.zeros((3, 16), np.float32)
    three[0, :8] = lin[:, 0]
    three[1, :8] = lin[:, 1]
    three[1, 8:] = lin[:, 0]
    three[2, 8:] = lin[:, 1]
    corner = np.zeros((128, 256), np.float32)
    for layer in range(3):
        for yv in range(3):
            for xv in range(3):
                corner[layer * 16 + yv * 4 + xv] = np.kron(three[xv], three[yv])
    wz = np.zeros((nw, nz), np.float32)
    for v in range(nw):
        wz[v, v * 8 : v * 8 + 8] += lin[:, 0]
        back = (v - 1) % nw
        wz[v, back * 8 : back * 8 + 8] += lin[:, 1]
    wz3 = np.concatenate([np.roll(wz, 1, axis=0), wz, np.roll(wz, -1, axis=0)], axis=0)
    nb = 2 * (2 * nw // BS)
    rep = np.kron(np.eye(nb, dtype=np.float32), np.ones((1, 8), np.float32))
    pick = np.zeros((2 * nw, 8), np.float32)
    for par in range(2):
        for w in range(nw):
            pick[par * nw + w, 2 * (w % 4) + par] = 1.0
    return deriv, (
        jnp.asarray(z_tables),
        jnp.asarray(y_table),
        jnp.asarray(corner[:64]),
        jnp.asarray(wz3),
        jnp.asarray(rep),
        jnp.asarray(pick),
        jnp.asarray(np.ascontiguousarray(corner[:16].T)),
    )


def halves(value):
    high = value.astype(BF16)
    return high, (value - high.astype(F32)).astype(BF16)


def mm(a, b, transposed=False):
    dims = (((1,), (1 if transposed else 0,)), ((), ()))
    dot = functools.partial(lax.dot_general, dimension_numbers=dims, preferred_element_type=F32)
    ah, al = halves(a)
    bh, bl = halves(b)
    return dot(ah, bh) + (dot(al, bh) + dot(ah, bl))


def kernel(
    nw, nd, deriv,
    *refs,
):
    sources, (out_ref, product_ref), held = refs[:13], refs[13:15], refs[15:28]
    (
        rhs_ref, metric_ref, helm_ref, columns_ref, live_ref, values_ref,
        zt_ref, yt_ref, corner_ref, wz3_ref, rep_ref, pick_ref, expand_ref,
    ) = held
    (
    xs, ys, es, xr, yr, er, qs, qr, cs, cr, inv_ref, m_ref, spread_ref,
    face_send, face_recv, q_send, q_recv, c_send, c_recv, load_sem,
    ) = refs[28:]
    loads = [
        pltpu.make_async_copy(source, target, load_sem.at[index])
        for index, (source, target) in enumerate(zip(sources, held))
    ]
    for index in (1, 0, 2, 6, 7, 5, 3, 4, 8, 9, 10, 11, 12):
        loads[index].start()
    nz = rhs_ref.shape[2]
    nxb = 2 * nw // BS
    nb = 2 * nxb
    width = nb * 8
    w = lax.axis_index("wide")
    d = lax.axis_index("deep")
    left, right = lax.rem(w + nw - 1, nw), lax.rem(w + 1, nw)
    down, up = lax.rem(d + nd - 1, nd), lax.rem(d + 1, nd)
    around = [up] if nd == 2 else [down, up]

    barrier = pltpu.get_barrier_semaphore()

    def greet(step, carry):
        to = lax.rem(w + step, nw)
        for other in around:
            pl.semaphore_signal(
                barrier, inc=1, device_id={"wide": to, "deep": other}, device_id_type=MESH
            )

        @pl.when(step > 0)
        def _():
            pl.semaphore_signal(
                barrier, inc=1, device_id={"wide": to, "deep": d}, device_id_type=MESH
            )

        return carry

    lax.fori_loop(0, nw, greet, 0)

    rows = lax.broadcasted_iota(jnp.int32, (16, 8, nz), 1)
    lanes = lax.broadcasted_iota(jnp.int32, (16, 16, nz), 2) % 8
    plane = lax.broadcasted_iota(jnp.int32, (16, nz), 0)

    def local_sum(f):
        after = pltpu.roll(f.reshape(256, nz), nz - 1, 1).reshape(16, 16, nz)
        before = pltpu.roll(f.reshape(256, nz), 1, 1).reshape(16, 16, nz)
        f = f + jnp.where(lanes == 7, after, jnp.where(lanes == 0, before, 0.0))
        lo, hi = f[:, :8], f[:, 8:]
        new_lo = lo + jnp.where(rows == 7, pltpu.roll(hi, 7, 1), 0.0)
        new_hi = hi + jnp.where(rows == 0, pltpu.roll(lo, 1, 1), 0.0)
        f = jnp.concatenate([new_lo, new_hi], axis=1)
        shared = f[7:8] + f[8:9]
        return jnp.concatenate([f[:7], shared, shared, f[9:]], axis=0)

    def face_copies(turn):
        pairs = [
            (xs.at[turn, 1], xr.at[turn, 0], right, d),
            (xs.at[turn, 0], xr.at[turn, 1], left, d),
            (ys.at[turn, 1], yr.at[turn, 0], w, up),
            (ys.at[turn, 0], yr.at[turn, 1], w, down),
            (es.at[turn, 3], er.at[turn, 0], right, up),
            (es.at[turn, 2], er.at[turn, 1], right, down),
            (es.at[turn, 1], er.at[turn, 2], left, up),
            (es.at[turn, 0], er.at[turn, 3], left, down),
        ]
        return [
            pltpu.make_async_remote_copy(
                src_ref=src,
                dst_ref=dst,
                send_sem=face_send.at[turn, index],
                recv_sem=face_recv.at[turn, index],
                device_id={"wide": to_w, "deep": to_d},
                device_id_type=MESH,
            )
            for index, (src, dst, to_w, to_d) in enumerate(pairs)
        ]

    def begin(turn, f):
        f = local_sum(f)
        xs[turn, 0] = f[0]
        xs[turn, 1] = f[15]
        ys[turn, 0] = f[:, 0:1]
        ys[turn, 1] = f[:, 15:16]
        es[turn, 0] = f[0, 0:1]
        es[turn, 1] = f[0, 15:16]
        es[turn, 2] = f[15, 0:1]
        es[turn, 3] = f[15, 15:16]
        copies = face_copies(turn)
        for copy in copies:
            copy.start()
        return f, copies

    def finish(turn, f, copies):
        for copy in copies:
            copy.wait_recv()
        lo = f[:, :8] + jnp.where(rows == 0, yr[turn, 0], 0.0)
        hi = f[:, 8:] + jnp.where(rows == 7, yr[turn, 1], 0.0)
        f = jnp.concatenate([lo, hi], axis=1)

        def face(side):
            edge_lo, edge_hi = er[turn, 2 * side], er[turn, 2 * side + 1]
            return xr[turn, side] + jnp.where(
                plane == 0, edge_lo, jnp.where(plane == 15, edge_hi, 0.0)
            )

        return jnp.concatenate(
            [f[:1] + face(0)[None], f[1:15], f[15:] + face(1)[None]], axis=0
        )

    def x_apply(u, table):
        parts = u.reshape(2, 8, 16, nz)
        nodes = [parts[:, i] for i in range(8)]
        result = []
        for m in range(8):
            total = float(table[m, 0]) * nodes[0]
            for i in range(1, 8):
                total = total + float(table[m, i]) * nodes[i]
            result.append(total)
        return jnp.stack(result, axis=1).reshape(16, 16, nz)

    def y_apply(u, which):
        parts = u.reshape(32, 8, nz)

        def coefficient(shift):
            table = yt_ref[which, shift]
            if nz > 128:
                table = jnp.concatenate([table] * (nz // 128), axis=1)
            return table[None]

        total = coefficient(0) * parts
        for shift in range(1, 8):
            total = total + coefficient(shift) * pltpu.roll(parts, shift, 1)
        return total.reshape(16, 16, nz)

    def z_apply(u, which):
        flat = u.reshape(256, nz)
        result = []
        for start in range(0, nz, 128):
            high, low = halves(flat[:, start : start + 128])
            both = jnp.dot(
                jnp.concatenate([high, low], axis=1), zt_ref[which], preferred_element_type=F32
            )
            result.append(both[:, :128] + both[:, 128:])
        whole = result[0] if len(result) == 1 else jnp.concatenate(result, axis=1)
        return whole.reshape(16, 16, nz)

    def operator(u):
        total = helm_ref[...] * u
        total = total + x_apply(metric_ref[0] * x_apply(u, deriv), deriv.T)
        total = total + y_apply(metric_ref[1] * y_apply(u, 0), 1)
        return total + z_apply(metric_ref[2] * z_apply(u, 0), 1)

    for index in (1, 0, 2, 6, 7):
        loads[index].wait()
    square = deriv * deriv
    diagonal = helm_ref[...] + x_apply(metric_ref[0], square.T)
    diagonal = diagonal + y_apply(metric_ref[1], 2) + z_apply(metric_ref[2], 2)

    pl.semaphore_wait(barrier, nw * (1 + len(around)) - 1)
    diagonal, diagonal_copies = begin(0, diagonal)
    summed, rhs_copies = begin(1, rhs_ref[...])

    for index in (5, 3, 4, 8, 9, 10, 11, 12):
        loads[index].wait()

    v = jnp.concatenate([values_ref[0, y] for y in range(2)], axis=0)
    spread = mm(v.T, rep_ref[...]).reshape(K, BS, BS, width)
    slot_lane = lax.broadcasted_iota(jnp.int32, (BS, width), 1) % 8
    cols = jnp.concatenate([columns_ref[0, y] for y in range(2)], axis=0).astype(F32)
    live = jnp.concatenate(
        [jnp.concatenate([live_ref[0, y : y + 1, b : b + 1] for b in range(nxb)], axis=0) for y in range(2)],
        axis=0,
    )
    slot = lax.broadcasted_iota(jnp.int32, (nb, K), 1)
    cols = jnp.where(slot < live, cols, -1.0)
    cols = jnp.dot(
        cols.T.astype(BF16), rep_ref[...].astype(BF16), preferred_element_type=F32
    ).astype(jnp.int32)
    block = lax.broadcasted_iota(jnp.int32, (nw, width), 0) // 4
    sums = [jnp.zeros((nw, width), F32) for _ in range(12)]
    for k in range(K):
        chosen = jnp.zeros((BS, width), F32)
        for i in range(BS):
            chosen = chosen + jnp.where(slot_lane == i, spread[k, i], 0.0)
        placed = mm(pick_ref[...], chosen)
        for layer in range(3):
            for y in range(2):
                hit = cols[k : k + 1] == block + (layer * nb + y * nxb)
                for par in range(2):
                    at = layer * 4 + y * 2 + par
                    sums[at] = sums[at] + jnp.where(
                        hit, placed[par * nw : (par + 1) * nw], 0.0
                    )
    for at in range(12):
        m_ref[at] = sums[at]

    vertex = lax.broadcasted_iota(jnp.int32, (16, 2 * width), 0)
    lane = lax.broadcasted_iota(jnp.int32, (16, 2 * width), 1)
    yv, xv = vertex // 4, vertex % 4
    wanted_x = lax.rem(2 * w + xv, 2 * nw)
    wanted = jnp.where(yv < 2, yv * 2 * nw, width) + wanted_x
    selected = jnp.where((lane == wanted) & (yv < 3) & (xv < 3), 1.0, 0.0)
    spread_ref[...] = mm(expand_ref[...], selected)

    inverse = 1.0 / finish(0, diagonal, diagonal_copies)
    inv_ref[...] = inverse
    residual = finish(1, summed, rhs_copies)
    update = inverse * residual * (1.0 / centre)
    u = update
    f, face_two = begin(2, rhs_ref[...] - operator(u))
    residual = finish(2, f, face_two)
    update = (second_weight * first_weight) * update + (
        (2.0 * second_weight / half_width) * inv_ref[...]
    ) * residual
    first = u + update

    local_res = rhs_ref[...] - operator(first)
    vertices = mm(corner_ref[...], local_res.reshape(256, nz))
    shifted = mm(wz3_ref[...], vertices, True)
    group = lax.broadcasted_iota(jnp.int32, (nw, 64), 1) // 16
    packed = jnp.where(
        group == 0,
        shifted[:nw],
        jnp.where(group == 1, shifted[nw : 2 * nw], shifted[2 * nw :]),
    )
    packed = jnp.concatenate([packed, jnp.zeros((nw, 64), F32)], axis=1)
    for row in range(nw):
        qs[row] = packed[row : row + 1]
    qr[0, w] = qs[w]

    def q_copy(to, to_d, which):
        return pltpu.make_async_remote_copy(
            src_ref=qs.at[to],
            dst_ref=qr.at[which, w],
            send_sem=q_send.at[which],
            recv_sem=q_recv.at[which],
            device_id={"wide": to, "deep": to_d},
            device_id_type=MESH,
        )

    def q_start(step, carry):
        to = lax.rem(w + step, nw)
        q_copy(to, up, 1).start()

        @pl.when(step > 0)
        def _():
            q_copy(to, d, 0).start()

        return carry

    lax.fori_loop(0, nw, q_start, 0)

    def wait_rows(ref, count, which, semaphore):
        view = ref.at[which, pl.ds(0, count)]
        pltpu.make_async_copy(view, view, semaphore).wait()

    wait_rows(qr, nw - 1, 0, q_recv.at[0])
    wait_rows(qr, nw, 1, q_recv.at[1])
    own = jnp.concatenate([qr[0, row] for row in range(nw)], axis=0)
    below = jnp.concatenate([qr[1, row] for row in range(nw)], axis=0)
    frame = own + pltpu.roll(below, 128 - 8, 1)
    frame = frame + pltpu.roll(pltpu.roll(frame, 1, 0), 128 - 2, 1)
    total = jnp.zeros((nw, width), F32)
    for layer in range(3):
        for y in range(2):
            for par in range(2):
                at = layer * 16 + y * 4 + par
                total = total + m_ref[layer * 4 + y * 2 + par] * frame[:, at : at + 1]
    product = jnp.sum(total, axis=0, keepdims=True)
    cs[0] = product
    cr[0, w] = product
    product_ref[0, 0:1] = product[:, : 2 * nw]
    product_ref[0, 1:2] = product[:, 2 * nw :]

    def c_copy(to, to_d, which):
        return pltpu.make_async_remote_copy(
            src_ref=cs.at[0],
            dst_ref=cr.at[which, w],
            send_sem=c_send.at[which],
            recv_sem=c_recv.at[which],
            device_id={"wide": to, "deep": to_d},
            device_id_type=MESH,
        )

    def c_start(step, carry):
        to = lax.rem(w + step, nw)
        c_copy(to, down, 1).start()

        @pl.when(step > 0)
        def _():
            c_copy(to, d, 0).start()

        return carry

    lax.fori_loop(0, nw, c_start, 0)
    wait_rows(cr, nw - 1, 0, c_recv.at[0])
    wait_rows(cr, nw, 1, c_recv.at[1])
    mine = jnp.concatenate([cr[0, row] for row in range(nw)], axis=0)
    above = jnp.concatenate([cr[1, row] for row in range(nw)], axis=0)
    both = jnp.concatenate([mine, above], axis=1)
    correction = mm(mm(spread_ref[...], both, True), wz3_ref[nw : 2 * nw])
    u = first + correction.reshape(16, 16, nz)

    f, face_three = begin(3, rhs_ref[...] - operator(u))
    update = inv_ref[...] * finish(3, f, face_three) * (1.0 / centre)
    u = u + update
    f, face_four = begin(4, rhs_ref[...] - operator(u))
    residual = finish(4, f, face_four)
    update = (second_weight * first_weight) * update + (
        (2.0 * second_weight / half_width) * inv_ref[...]
    ) * residual
    out_ref[...] = u + update

    for copies in (diagonal_copies, rhs_copies, face_two, face_three, face_four):
        for copy in copies:
            copy.wait_send()
    wait_rows(qr, nw - 1, 0, q_send.at[0])
    wait_rows(qr, nw, 1, q_send.at[1])
    wait_rows(cr, nw - 1, 0, c_send.at[0])
    wait_rows(cr, nw, 1, c_send.at[1])


def local(nw, nd, *arguments):
    rhs = arguments[0]
    nz = rhs.shape[2]
    deriv, tables = tables_of(nw, nz)
    width = 4 * nw
    vmem = pl.BlockSpec(memory_space=pltpu.VMEM)
    return pl.pallas_call(
        functools.partial(kernel, nw, nd, deriv),
        out_shape=(
            jax.ShapeDtypeStruct(rhs.shape, F32),
            jax.ShapeDtypeStruct((1, 2, 2 * nw), F32),
        ),
        in_specs=[pl.BlockSpec(memory_space=pltpu.HBM)] * 13,
        out_specs=(vmem, vmem),
        scratch_shapes=[pltpu.VMEM(a.shape, a.dtype) for a in (*arguments, *tables)]
        + [
            pltpu.VMEM((5, 2, 16, nz), F32),
            pltpu.VMEM((5, 2, 16, 1, nz), F32),
            pltpu.VMEM((5, 4, 1, nz), F32),
            pltpu.VMEM((5, 2, 16, nz), F32),
            pltpu.VMEM((5, 2, 16, 1, nz), F32),
            pltpu.VMEM((5, 4, 1, nz), F32),
            pltpu.VMEM((nw, 1, 128), F32),
            pltpu.VMEM((2, nw, 1, 128), F32),
            pltpu.VMEM((1, 1, width), F32),
            pltpu.VMEM((2, nw, 1, width), F32),
            pltpu.VMEM((16, 16, nz), F32),
            pltpu.VMEM((12, nw, width), F32),
            pltpu.VMEM((256, 2 * width), F32),
            pltpu.SemaphoreType.DMA((5, 8)),
            pltpu.SemaphoreType.DMA((5, 8)),
            pltpu.SemaphoreType.DMA((2,)),
            pltpu.SemaphoreType.DMA((2,)),
            pltpu.SemaphoreType.DMA((2,)),
            pltpu.SemaphoreType.DMA((2,)),
            pltpu.SemaphoreType.DMA((13,)),
        ],
        compiler_params=pltpu.CompilerParams(
            collective_id=0, has_side_effects=True, vmem_limit_bytes=63 * 1024 * 1024
        ),
    )(*arguments, *tables)


def solution(mesh):
    placed = (
        P("wide", "deep", None),
        P(None, "wide", "deep", None),
        P("wide", "deep", None),
        P("wide", "deep", None, None),
        P("wide", "deep", None),
        P("wide", "deep", None, None),
    )
    return jax.shard_map(
        functools.partial(local, mesh.shape["wide"], mesh.shape["deep"]),
        mesh=mesh,
        in_specs=placed,
        out_specs=(P("wide", "deep", None), P("wide", "deep", None)),
        check_vma=False,
    )
```

```python
import functools

import jax
import jax.numpy as jnp
import numpy as np
from jax import lax
from jax.experimental import pallas as pl
from jax.experimental.pallas import tpu as pltpu
from jax.sharding import PartitionSpec as P

NP = 8
K = 8
BS = 8
MESH = pl.DeviceIdType.MESH
F32 = jnp.float32
BF16 = jnp.bfloat16

upper_bound = 6.0
lower_bound = 0.6
centre = (upper_bound + lower_bound) / 2.0
half_width = (upper_bound - lower_bound) / 2.0
aspect = centre / half_width
first_weight = 1.0 / aspect
second_weight = 1.0 / (2.0 * aspect - first_weight)


def gll_tables(count):
    order = count - 1
    nodes = np.cos(np.pi * np.arange(count) / order)
    legendre = np.zeros((count, count))
    for sweep in range(101):
        legendre[:, 0] = 1.0
        legendre[:, 1] = nodes
        for degree in range(2, count):
            legendre[:, degree] = (
                (2 * degree - 1) * nodes * legendre[:, degree - 1]
                - (degree - 1) * legendre[:, degree - 2]
            ) / degree
        if sweep < 100:
            nodes = nodes - (nodes * legendre[:, order] - legendre[:, order - 1]) / (
                count * legendre[:, order]
            )
    nodes = nodes[::-1].copy()
    values = legendre[::-1, order].copy()
    identity_table = np.eye(count)
    spacing = nodes[:, None] - nodes[None, :] + identity_table
    derivative = values[:, None] / values[None, :] / spacing
    derivative = derivative * (1.0 - identity_table)
    derivative[0, 0] = -order * (order + 1) / 4.0
    derivative[-1, -1] = order * (order + 1) / 4.0
    linear = np.stack([(1.0 - nodes) / 2.0, (1.0 + nodes) / 2.0], axis=1)
    return derivative.astype(np.float32), linear.astype(np.float32)


def stacked_pieces(table):
    high = table.astype(jnp.bfloat16)
    low = (table - high.astype(np.float32)).astype(jnp.bfloat16)
    row = np.concatenate([high, low], axis=1)
    return np.concatenate([row, row], axis=0)


def tables_of(nw, nz):
    deriv, lin = gll_tables(NP)
    eye = np.eye(16, dtype=np.float32)
    square = deriv * deriv
    z_tables = np.stack(
        [
            stacked_pieces(np.kron(eye, deriv.T)),
            stacked_pieces(np.kron(eye, deriv)),
            stacked_pieces(np.kron(eye, square)),
        ]
    )
    node = np.arange(8)
    y_table = np.zeros((3, 8, 8, 128), np.float32)
    for shift in range(8):
        other = (node - shift) % 8
        y_table[0, shift] = deriv[node, other][:, None]
        y_table[1, shift] = deriv[other, node][:, None]
        y_table[2, shift] = square[other, node][:, None]
    three = np.zeros((3, 16), np.float32)
    three[0, :8] = lin[:, 0]
    three[1, :8] = lin[:, 1]
    three[1, 8:] = lin[:, 0]
    three[2, 8:] = lin[:, 1]
    corner = np.zeros((128, 256), np.float32)
    for layer in range(3):
        for yv in range(3):
            for xv in range(3):
                corner[layer * 16 + yv * 4 + xv] = np.kron(three[xv], three[yv])
    five = np.zeros((5, 32), np.float32)
    for element in range(4):
        five[element, element * 8 : element * 8 + 8] = lin[:, 0]
        five[element + 1, element * 8 : element * 8 + 8] = lin[:, 1]
    expand = np.zeros((512, 32), np.float32)
    for yv in range(3):
        for xv in range(5):
            expand[:, yv * 8 + xv] = np.kron(five[xv], three[yv])
    wz = np.zeros((nw, nz), np.float32)
    for v in range(nw):
        wz[v, v * 8 : v * 8 + 8] += lin[:, 0]
        back = (v - 1) % nw
        wz[v, back * 8 : back * 8 + 8] += lin[:, 1]
    wz3 = np.concatenate([np.roll(wz, 1, axis=0), wz, np.roll(wz, -1, axis=0)], axis=0)
    nb = 2 * (2 * nw // BS)
    rep = np.kron(np.eye(nb, dtype=np.float32), np.ones((1, 8), np.float32))
    pick = np.zeros((2 * nw, 8), np.float32)
    for par in range(2):
        for w in range(nw):
            pick[par * nw + w, 2 * (w % 4) + par] = 1.0
    return deriv, (
        jnp.asarray(z_tables),
        jnp.asarray(y_table),
        jnp.asarray(corner[:64]),
        jnp.asarray(wz3),
        jnp.asarray(rep),
        jnp.asarray(pick),
        jnp.asarray(expand),
    )


def halves(value):
    high = value.astype(BF16)
    return high, (value - high.astype(F32)).astype(BF16)


def mm(a, b, transposed=False):
    dims = (((1,), (1 if transposed else 0,)), ((), ()))
    dot = functools.partial(lax.dot_general, dimension_numbers=dims, preferred_element_type=F32)
    ah, al = halves(a)
    bh, bl = halves(b)
    return dot(ah, bh) + (dot(al, bh) + dot(ah, bl))


def kernel(
    nw, nd, deriv,
    *refs,
):
    sources, (out_ref, product_ref), held = refs[:13], refs[13:15], refs[15:28]
    (
        rhs_ref, metric_ref, helm_ref, columns_ref, live_ref, values_ref,
        zt_ref, yt_ref, corner_ref, wz3_ref, rep_ref, pick_ref, expand_ref,
    ) = held
    (
    xs, ys, es, xr, yr, er, qs, qr, cs, cr, gm, ls, lr, inv_ref, m_ref, spread_ref,
    face_send, face_recv, q_send, q_recv, c_send, c_recv, ghost_send, ghost_recv, load_sem,
    ) = refs[28:]
    loads = [
        pltpu.make_async_copy(source, target, load_sem.at[index])
        for index, (source, target) in enumerate(zip(sources, held))
    ]
    for index in (1, 0, 2, 6, 7, 5, 3, 4, 8, 9, 10, 11, 12):
        loads[index].start()
    nz = rhs_ref.shape[2]
    nxb = 2 * nw // BS
    nb = 2 * nxb
    width = nb * 8
    w = lax.axis_index("wide")
    d = lax.axis_index("deep")
    left, right = lax.rem(w + nw - 1, nw), lax.rem(w + 1, nw)
    down, up = lax.rem(d + nd - 1, nd), lax.rem(d + 1, nd)
    around = [up] if nd == 2 else [down, up]

    barrier = pltpu.get_barrier_semaphore()

    def greet(step, carry):
        to = lax.rem(w + step, nw)
        for other in around:
            pl.semaphore_signal(
                barrier, inc=1, device_id={"wide": to, "deep": other}, device_id_type=MESH
            )

        @pl.when(step > 0)
        def _():
            pl.semaphore_signal(
                barrier, inc=1, device_id={"wide": to, "deep": d}, device_id_type=MESH
            )

        return carry

    lax.fori_loop(0, nw, greet, 0)

    row = lax.broadcasted_iota(jnp.int32, (1, 8, nz), 1)
    lanes = lax.broadcasted_iota(jnp.int32, (1, 16, nz), 2) % 8
    plane = lax.broadcasted_iota(jnp.int32, (16, nz), 0)

    def plane_sum(f):
        count = f.shape[0]
        flat = f.reshape(count * 16, nz)
        after = pltpu.roll(flat, nz - 1, 1).reshape(count, 16, nz)
        before = pltpu.roll(flat, 1, 1).reshape(count, 16, nz)
        f = f + jnp.where(lanes == 7, after, jnp.where(lanes == 0, before, 0.0))
        lo, hi = f[:, :8], f[:, 8:]
        new_lo = lo + jnp.where(row == 7, pltpu.roll(hi, 7, 1), 0.0)
        new_hi = hi + jnp.where(row == 0, pltpu.roll(lo, 1, 1), 0.0)
        return jnp.concatenate([new_lo, new_hi], axis=1)

    def local_sum(f):
        f = plane_sum(f)
        shared = f[7:8] + f[8:9]
        return jnp.concatenate([f[:7], shared, shared, f[9:]], axis=0)

    def face_copies(turn):
        pairs = [
            (xs.at[turn, 1], xr.at[turn, 0], right, d),
            (xs.at[turn, 0], xr.at[turn, 1], left, d),
            (ys.at[turn, 1, pl.ds(0, 16)], yr.at[turn, 0, pl.ds(0, 16)], w, up),
            (ys.at[turn, 0, pl.ds(0, 16)], yr.at[turn, 1, pl.ds(0, 16)], w, down),
            (es.at[turn, 3], er.at[turn, 0], right, up),
            (es.at[turn, 2], er.at[turn, 1], right, down),
            (es.at[turn, 1], er.at[turn, 2], left, up),
            (es.at[turn, 0], er.at[turn, 3], left, down),
        ]
        return [
            pltpu.make_async_remote_copy(
                src_ref=src,
                dst_ref=dst,
                send_sem=face_send.at[turn, index],
                recv_sem=face_recv.at[turn, index],
                device_id={"wide": to_w, "deep": to_d},
                device_id_type=MESH,
            )
            for index, (src, dst, to_w, to_d) in enumerate(pairs)
        ]

    def begin(turn, f):
        f = local_sum(f)
        xs[turn, 0] = f[0]
        xs[turn, 1] = f[15]
        ys[turn, 0, 0:16] = f[:, 0:1]
        ys[turn, 1, 0:16] = f[:, 15:16]
        es[turn, 0] = f[0, 0:1]
        es[turn, 1] = f[0, 15:16]
        es[turn, 2] = f[15, 0:1]
        es[turn, 3] = f[15, 15:16]
        copies = face_copies(turn)
        for copy in copies:
            copy.start()
        return f, copies

    def add_rows(f, low, high):
        lo = f[:, :8] + jnp.where(row == 0, low, 0.0)
        hi = f[:, 8:] + jnp.where(row == 7, high, 0.0)
        return jnp.concatenate([lo, hi], axis=1)

    def ghost_copy(index, src, dst, to):
        return pltpu.make_async_remote_copy(
            src_ref=src,
            dst_ref=dst,
            send_sem=ghost_send.at[index],
            recv_sem=ghost_recv.at[index],
            device_id={"wide": to, "deep": d},
            device_id_type=MESH,
        )

    def ghost_copies():
        result = []
        for side, (to, start, face) in enumerate(((right, 8, 15), (left, 0, 0))):
            pieces = (
                (metric_ref.at[0, pl.ds(start, 8)], gm.at[side, pl.ds(0, 8)]),
                (metric_ref.at[1, face], gm.at[side, 8]),
                (metric_ref.at[2, face], gm.at[side, 9]),
                (helm_ref.at[face], gm.at[side, 10]),
            )
            for index, (src, dst) in enumerate(pieces):
                result.append(ghost_copy(side * 5 + index, src, dst, to))
        return result

    def finish(turn, f, copies):
        for copy in copies:
            copy.wait_recv()
        f = add_rows(f, yr[turn, 0, 0:16], yr[turn, 1, 0:16])

        def face(side):
            edge_lo, edge_hi = er[turn, 2 * side], er[turn, 2 * side + 1]
            return xr[turn, side] + jnp.where(
                plane == 0, edge_lo, jnp.where(plane == 15, edge_hi, 0.0)
            )

        return jnp.concatenate(
            [f[:1] + face(0)[None], f[1:15], f[15:] + face(1)[None]], axis=0
        )

    def x_apply(u, table):
        parts = u.reshape(2, 8, 16, nz)
        nodes = [parts[:, i] for i in range(8)]
        result = []
        for m in range(8):
            total = float(table[m, 0]) * nodes[0]
            for i in range(1, 8):
                total = total + float(table[m, i]) * nodes[i]
            result.append(total)
        return jnp.stack(result, axis=1).reshape(16, 16, nz)

    def y_apply(u, which):
        parts = u.reshape(-1, 8, nz)

        def coefficient(shift):
            table = yt_ref[which, shift]
            if nz > 128:
                table = jnp.concatenate([table] * (nz // 128), axis=1)
            return table[None]

        total = coefficient(0) * parts
        for shift in range(1, 8):
            total = total + coefficient(shift) * pltpu.roll(parts, shift, 1)
        return total.reshape(u.shape)

    def z_apply(u, which):
        flat = u.reshape(-1, nz)
        result = []
        for start in range(0, nz, 128):
            high, low = halves(flat[:, start : start + 128])
            both = jnp.dot(
                jnp.concatenate([high, low], axis=1), zt_ref[which], preferred_element_type=F32
            )
            result.append(both[:, :128] + both[:, 128:])
        whole = result[0] if len(result) == 1 else jnp.concatenate(result, axis=1)
        return whole.reshape(u.shape)

    def operator(u):
        total = helm_ref[...] * u
        total = total + x_apply(metric_ref[0] * x_apply(u, deriv), deriv.T)
        total = total + y_apply(metric_ref[1] * y_apply(u, 0), 1)
        return total + z_apply(metric_ref[2] * z_apply(u, 0), 1)

    for index in (1, 0, 2, 6, 7):
        loads[index].wait()
    def ghost_face(side, u, face):
        nodes = [u[i] for i in range(8)]
        total = gm[side, 10] * nodes[face]
        for m in range(8):
            slope = float(deriv[m, 0]) * nodes[0]
            for i in range(1, 8):
                slope = slope + float(deriv[m, i]) * nodes[i]
            total = total + float(deriv[m, face]) * (gm[side, m] * slope)
        total = total + y_apply(gm[side, 8] * y_apply(nodes[face], 0), 1)
        total = total + z_apply(gm[side, 9] * z_apply(nodes[face], 0), 1)
        return lr[side] - total

    square = deriv * deriv
    diagonal = helm_ref[...] + x_apply(metric_ref[0], square.T)
    diagonal = diagonal + y_apply(metric_ref[1], 2) + z_apply(metric_ref[2], 2)

    pl.semaphore_wait(barrier, nw * (1 + len(around)) - 1)
    diagonal, diagonal_copies = begin(0, diagonal)
    summed, rhs_copies = begin(1, rhs_ref[...])

    for index in (5, 3, 4, 8, 9, 10, 11, 12):
        loads[index].wait()

    v = jnp.concatenate([values_ref[0, y] for y in range(2)], axis=0)
    spread = mm(v.T, rep_ref[...]).reshape(K, BS, BS, width)
    slot_lane = lax.broadcasted_iota(jnp.int32, (BS, width), 1) % 8
    cols = jnp.concatenate([columns_ref[0, y] for y in range(2)], axis=0).astype(F32)
    live = jnp.concatenate(
        [jnp.concatenate([live_ref[0, y : y + 1, b : b + 1] for b in range(nxb)], axis=0) for y in range(2)],
        axis=0,
    )
    slot = lax.broadcasted_iota(jnp.int32, (nb, K), 1)
    cols = jnp.where(slot < live, cols, -1.0)
    cols = jnp.dot(
        cols.T.astype(BF16), rep_ref[...].astype(BF16), preferred_element_type=F32
    ).astype(jnp.int32)
    block = lax.broadcasted_iota(jnp.int32, (nw, width), 0) // 4
    sums = [jnp.zeros((nw, width), F32) for _ in range(12)]
    for k in range(K):
        chosen = jnp.zeros((BS, width), F32)
        for i in range(BS):
            chosen = chosen + jnp.where(slot_lane == i, spread[k, i], 0.0)
        placed = mm(pick_ref[...], chosen)
        for layer in range(3):
            for y in range(2):
                hit = cols[k : k + 1] == block + (layer * nb + y * nxb)
                for par in range(2):
                    at = layer * 4 + y * 2 + par
                    sums[at] = sums[at] + jnp.where(
                        hit, placed[par * nw : (par + 1) * nw], 0.0
                    )
    for at in range(12):
        m_ref[at] = sums[at]

    vertex = lax.broadcasted_iota(jnp.int32, (32, 2 * width), 0)
    lane = lax.broadcasted_iota(jnp.int32, (32, 2 * width), 1)
    yv, xv = vertex // 8, vertex % 8
    wanted_x = lax.rem(2 * w - 1 + xv + 2 * nw, 2 * nw)
    wanted = jnp.where(yv < 2, yv * 2 * nw, width) + wanted_x
    selected = jnp.where((lane == wanted) & (yv < 3) & (xv < 5), 1.0, 0.0)
    spread_ref[...] = mm(expand_ref[...], selected)

    inverse = 1.0 / finish(0, diagonal, diagonal_copies)
    inv_ref[...] = inverse
    residual = finish(1, summed, rhs_copies)
    update = inverse * residual * (1.0 / centre)
    u = update
    f, face_two = begin(2, rhs_ref[...] - operator(u))
    ghosts = ghost_copies()
    for ghost in ghosts:
        ghost.start()
    residual = finish(2, f, face_two)
    update = (second_weight * first_weight) * update + (
        (2.0 * second_weight / half_width) * inv_ref[...]
    ) * residual
    first = u + update

    local_res = rhs_ref[...] - operator(first)
    vertices = mm(corner_ref[...], local_res.reshape(256, nz))
    shifted = mm(wz3_ref[...], vertices, True)
    group = lax.broadcasted_iota(jnp.int32, (nw, 64), 1) // 16
    packed = jnp.where(
        group == 0,
        shifted[:nw],
        jnp.where(group == 1, shifted[nw : 2 * nw], shifted[2 * nw :]),
    )
    packed = jnp.concatenate([packed, jnp.zeros((nw, 64), F32)], axis=1)
    for at in range(nw):
        qs[at] = packed[at : at + 1]
    qr[0, w] = qs[w]

    def q_copy(to, to_d, which):
        return pltpu.make_async_remote_copy(
            src_ref=qs.at[to],
            dst_ref=qr.at[which, w],
            send_sem=q_send.at[which],
            recv_sem=q_recv.at[which],
            device_id={"wide": to, "deep": to_d},
            device_id_type=MESH,
        )

    def q_start(step, carry):
        to = lax.rem(w + step, nw)
        q_copy(to, up, 1).start()

        @pl.when(step > 0)
        def _():
            q_copy(to, d, 0).start()

        return carry

    lax.fori_loop(0, nw, q_start, 0)
    ls[0] = local_res[0]
    ls[1] = local_res[15]
    faces = [ghost_copy(4, ls.at[1], lr.at[0], right), ghost_copy(9, ls.at[0], lr.at[1], left)]
    for ghost in faces:
        ghost.start()
    ghosts = ghosts + faces

    def wait_rows(ref, count, which, semaphore):
        view = ref.at[which, pl.ds(0, count)]
        pltpu.make_async_copy(view, view, semaphore).wait()

    wait_rows(qr, nw - 1, 0, q_recv.at[0])
    wait_rows(qr, nw, 1, q_recv.at[1])
    own = jnp.concatenate([qr[0, at] for at in range(nw)], axis=0)
    below = jnp.concatenate([qr[1, at] for at in range(nw)], axis=0)
    frame = own + pltpu.roll(below, 128 - 8, 1)
    frame = frame + pltpu.roll(pltpu.roll(frame, 1, 0), 128 - 2, 1)
    total = jnp.zeros((nw, width), F32)
    for layer in range(3):
        for y in range(2):
            for par in range(2):
                at = layer * 16 + y * 4 + par
                total = total + m_ref[layer * 4 + y * 2 + par] * frame[:, at : at + 1]
    product = jnp.sum(total, axis=0, keepdims=True)
    cs[0] = product
    cr[0, w] = product
    product_ref[0, 0:1] = product[:, : 2 * nw]
    product_ref[0, 1:2] = product[:, 2 * nw :]

    def c_copy(to, to_d, which):
        return pltpu.make_async_remote_copy(
            src_ref=cs.at[0],
            dst_ref=cr.at[which, w],
            send_sem=c_send.at[which],
            recv_sem=c_recv.at[which],
            device_id={"wide": to, "deep": to_d},
            device_id_type=MESH,
        )

    def c_start(step, carry):
        to = lax.rem(w + step, nw)
        c_copy(to, down, 1).start()

        @pl.when(step > 0)
        def _():
            c_copy(to, d, 0).start()

        return carry

    lax.fori_loop(0, nw, c_start, 0)
    wait_rows(cr, nw - 1, 0, c_recv.at[0])
    wait_rows(cr, nw, 1, c_recv.at[1])
    mine = jnp.concatenate([cr[0, at] for at in range(nw)], axis=0)
    above = jnp.concatenate([cr[1, at] for at in range(nw)], axis=0)
    both = jnp.concatenate([mine, above], axis=1)
    correction = mm(mm(spread_ref[...], both, True), wz3_ref[nw : 2 * nw])
    for ghost in ghosts:
        ghost.wait_recv()
    correction = correction.reshape(32, 16, nz)
    outer = jnp.stack(
        [ghost_face(0, correction[:8], 7), ghost_face(1, correction[24:], 0)], axis=0
    )
    outer = plane_sum(outer)
    correction = correction[8:24]
    u = first + correction
    f = local_sum(local_res - operator(correction))
    for side, edge in ((0, 0), (1, 15)):
        ys[3, side, 0:16] = f[:, edge : edge + 1]
        ys[3, side, 16:18] = outer[:, edge : edge + 1]
    face_three = [
        pltpu.make_async_remote_copy(
            src_ref=ys.at[3, 1 - side],
            dst_ref=yr.at[3, side],
            send_sem=face_send.at[3, side],
            recv_sem=face_recv.at[3, side],
            device_id={"wide": w, "deep": to},
            device_id_type=MESH,
        )
        for side, to in ((0, up), (1, down))
    ]
    for copy in face_three:
        copy.start()
    for copy in face_three:
        copy.wait_recv()
    outer = add_rows(outer, yr[3, 0, 16:18], yr[3, 1, 16:18])
    f = add_rows(f, yr[3, 0, 0:16], yr[3, 1, 0:16])
    f = jnp.concatenate([f[:1] + outer[:1], f[1:15], f[15:] + outer[1:]], axis=0)
    update = inv_ref[...] * f * (1.0 / centre)
    u = u + update
    f, face_four = begin(4, rhs_ref[...] - operator(u))
    residual = finish(4, f, face_four)
    update = (second_weight * first_weight) * update + (
        (2.0 * second_weight / half_width) * inv_ref[...]
    ) * residual
    out_ref[...] = u + update

    for copies in (diagonal_copies, rhs_copies, face_two, ghosts, face_three, face_four):
        for copy in copies:
            copy.wait_send()
    wait_rows(qr, nw - 1, 0, q_send.at[0])
    wait_rows(qr, nw, 1, q_send.at[1])
    wait_rows(cr, nw - 1, 0, c_send.at[0])
    wait_rows(cr, nw, 1, c_send.at[1])


def local(nw, nd, *arguments):
    rhs = arguments[0]
    nz = rhs.shape[2]
    deriv, tables = tables_of(nw, nz)
    width = 4 * nw
    vmem = pl.BlockSpec(memory_space=pltpu.VMEM)
    return pl.pallas_call(
        functools.partial(kernel, nw, nd, deriv),
        out_shape=(
            jax.ShapeDtypeStruct(rhs.shape, F32),
            jax.ShapeDtypeStruct((1, 2, 2 * nw), F32),
        ),
        in_specs=[pl.BlockSpec(memory_space=pltpu.HBM)] * 13,
        out_specs=(vmem, vmem),
        scratch_shapes=[pltpu.VMEM(a.shape, a.dtype) for a in (*arguments, *tables)]
        + [
            pltpu.VMEM((5, 2, 16, nz), F32),
            pltpu.VMEM((5, 2, 18, 1, nz), F32),
            pltpu.VMEM((5, 4, 1, nz), F32),
            pltpu.VMEM((5, 2, 16, nz), F32),
            pltpu.VMEM((5, 2, 18, 1, nz), F32),
            pltpu.VMEM((5, 4, 1, nz), F32),
            pltpu.VMEM((nw, 1, 128), F32),
            pltpu.VMEM((2, nw, 1, 128), F32),
            pltpu.VMEM((1, 1, width), F32),
            pltpu.VMEM((2, nw, 1, width), F32),
            pltpu.VMEM((2, 11, 16, nz), F32),
            pltpu.VMEM((2, 16, nz), F32),
            pltpu.VMEM((2, 16, nz), F32),
            pltpu.VMEM((16, 16, nz), F32),
            pltpu.VMEM((12, nw, width), F32),
            pltpu.VMEM((512, 2 * width), F32),
            pltpu.SemaphoreType.DMA((5, 8)),
            pltpu.SemaphoreType.DMA((5, 8)),
            pltpu.SemaphoreType.DMA((2,)),
            pltpu.SemaphoreType.DMA((2,)),
            pltpu.SemaphoreType.DMA((2,)),
            pltpu.SemaphoreType.DMA((2,)),
            pltpu.SemaphoreType.DMA((10,)),
            pltpu.SemaphoreType.DMA((10,)),
            pltpu.SemaphoreType.DMA((13,)),
        ],
        compiler_params=pltpu.CompilerParams(
            collective_id=0, has_side_effects=True, vmem_limit_bytes=63 * 1024 * 1024
        ),
    )(*arguments, *tables)


def solution(mesh):
    placed = (
        P("wide", "deep", None),
        P(None, "wide", "deep", None),
        P("wide", "deep", None),
        P("wide", "deep", None, None),
        P("wide", "deep", None),
        P("wide", "deep", None, None),
    )
    return jax.shard_map(
        functools.partial(local, mesh.shape["wide"], mesh.shape["deep"]),
        mesh=mesh,
        in_specs=placed,
        out_specs=(P("wide", "deep", None), P("wide", "deep", None)),
        check_vma=False,
    )
```

```python
import functools

import jax
import jax.numpy as jnp
import numpy as np
from jax import lax
from jax.experimental import pallas as pl
from jax.experimental.pallas import tpu as pltpu
from jax.sharding import PartitionSpec as P

NP = 8
K = 8
BS = 8
MESH = pl.DeviceIdType.MESH
F32 = jnp.float32
BF16 = jnp.bfloat16

upper_bound = 6.0
lower_bound = 0.6
centre = (upper_bound + lower_bound) / 2.0
half_width = (upper_bound - lower_bound) / 2.0
aspect = centre / half_width
first_weight = 1.0 / aspect
second_weight = 1.0 / (2.0 * aspect - first_weight)


def gll_tables(count):
    order = count - 1
    nodes = np.cos(np.pi * np.arange(count) / order)
    legendre = np.zeros((count, count))
    for sweep in range(101):
        legendre[:, 0] = 1.0
        legendre[:, 1] = nodes
        for degree in range(2, count):
            legendre[:, degree] = (
                (2 * degree - 1) * nodes * legendre[:, degree - 1]
                - (degree - 1) * legendre[:, degree - 2]
            ) / degree
        if sweep < 100:
            nodes = nodes - (nodes * legendre[:, order] - legendre[:, order - 1]) / (
                count * legendre[:, order]
            )
    nodes = nodes[::-1].copy()
    values = legendre[::-1, order].copy()
    identity_table = np.eye(count)
    spacing = nodes[:, None] - nodes[None, :] + identity_table
    derivative = values[:, None] / values[None, :] / spacing
    derivative = derivative * (1.0 - identity_table)
    derivative[0, 0] = -order * (order + 1) / 4.0
    derivative[-1, -1] = order * (order + 1) / 4.0
    linear = np.stack([(1.0 - nodes) / 2.0, (1.0 + nodes) / 2.0], axis=1)
    return derivative.astype(np.float32), linear.astype(np.float32)


def stacked_pieces(table):
    high = table.astype(jnp.bfloat16)
    low = (table - high.astype(np.float32)).astype(jnp.bfloat16)
    row = np.concatenate([high, low], axis=1)
    return np.concatenate([row, row], axis=0)


def tables_of(nw, nz):
    deriv, lin = gll_tables(NP)
    eye = np.eye(16, dtype=np.float32)
    square = deriv * deriv
    z_tables = np.stack(
        [
            stacked_pieces(np.kron(eye, deriv.T)),
            stacked_pieces(np.kron(eye, deriv)),
            stacked_pieces(np.kron(eye, square)),
        ]
    )
    node = np.arange(8)
    y_table = np.zeros((3, 8, 8, 128), np.float32)
    for shift in range(8):
        other = (node - shift) % 8
        y_table[0, shift] = deriv[node, other][:, None]
        y_table[1, shift] = deriv[other, node][:, None]
        y_table[2, shift] = square[other, node][:, None]
    three = np.zeros((3, 16), np.float32)
    three[0, :8] = lin[:, 0]
    three[1, :8] = lin[:, 1]
    three[1, 8:] = lin[:, 0]
    three[2, 8:] = lin[:, 1]
    corner = np.zeros((128, 256), np.float32)
    for layer in range(3):
        for yv in range(3):
            for xv in range(3):
                corner[layer * 16 + yv * 4 + xv] = np.kron(three[xv], three[yv])
    five = np.zeros((5, 32), np.float32)
    for element in range(4):
        five[element, element * 8 : element * 8 + 8] = lin[:, 0]
        five[element + 1, element * 8 : element * 8 + 8] = lin[:, 1]
    expand = np.zeros((512, 32), np.float32)
    for yv in range(3):
        for xv in range(5):
            expand[:, yv * 8 + xv] = np.kron(five[xv], three[yv])
    wz = np.zeros((nw, nz), np.float32)
    for v in range(nw):
        wz[v, v * 8 : v * 8 + 8] += lin[:, 0]
        back = (v - 1) % nw
        wz[v, back * 8 : back * 8 + 8] += lin[:, 1]
    wz3 = np.concatenate([np.roll(wz, 1, axis=0), wz, np.roll(wz, -1, axis=0)], axis=0)
    nb = 2 * (2 * nw // BS)
    rep = np.kron(np.eye(nb, dtype=np.float32), np.ones((1, 8), np.float32))
    pick = np.zeros((2 * nw, 8), np.float32)
    for par in range(2):
        for w in range(nw):
            pick[par * nw + w, 2 * (w % 4) + par] = 1.0
    return deriv, (
        jnp.asarray(z_tables),
        jnp.asarray(y_table),
        jnp.asarray(corner[:64]),
        jnp.asarray(wz3),
        jnp.asarray(rep),
        jnp.asarray(pick),
        jnp.asarray(expand),
    )


def halves(value):
    high = value.astype(BF16)
    return high, (value - high.astype(F32)).astype(BF16)


def mm(a, b, transposed=False):
    dims = (((1,), (1 if transposed else 0,)), ((), ()))
    dot = functools.partial(lax.dot_general, dimension_numbers=dims, preferred_element_type=F32)
    ah, al = halves(a)
    bh, bl = halves(b)
    return dot(ah, bh) + (dot(al, bh) + dot(ah, bl))


def kernel(
    nw, nd, deriv,
    *refs,
):
    sources, (out_ref, product_ref), held = refs[:13], refs[13:15], refs[15:28]
    (
        rhs_ref, metric_ref, helm_ref, columns_ref, live_ref, values_ref,
        zt_ref, yt_ref, corner_ref, wz3_ref, rep_ref, pick_ref, expand_ref,
    ) = held
    (
    xs, ys, es, xr, yr, er, qs, qr, cs, cr, gm, ls, lr, inv_ref, m_ref, spread_ref,
    face_send, face_recv, q_send, q_recv, c_send, c_recv, ghost_send, ghost_recv, load_sem,
    ) = refs[28:]
    loads = [
        pltpu.make_async_copy(source, target, load_sem.at[index])
        for index, (source, target) in enumerate(zip(sources, held))
    ]
    for index in (1, 0, 2, 6, 7, 5, 3, 4, 8, 9, 10, 11, 12):
        loads[index].start()
    nz = rhs_ref.shape[2]
    nxb = 2 * nw // BS
    nb = 2 * nxb
    width = nb * 8
    w = lax.axis_index("wide")
    d = lax.axis_index("deep")
    left, right = lax.rem(w + nw - 1, nw), lax.rem(w + 1, nw)
    down, up = lax.rem(d + nd - 1, nd), lax.rem(d + 1, nd)
    around = [up] if nd == 2 else [down, up]

    barrier = pltpu.get_barrier_semaphore()

    def greet(step, carry):
        to = lax.rem(w + step, nw)
        for other in around:
            pl.semaphore_signal(
                barrier, inc=1, device_id={"wide": to, "deep": other}, device_id_type=MESH
            )

        @pl.when(step > 0)
        def _():
            pl.semaphore_signal(
                barrier, inc=1, device_id={"wide": to, "deep": d}, device_id_type=MESH
            )

        return carry

    lax.fori_loop(0, nw, greet, 0)

    row = lax.broadcasted_iota(jnp.int32, (1, 8, nz), 1)
    lanes = lax.broadcasted_iota(jnp.int32, (1, 16, nz), 2) % 8
    plane = lax.broadcasted_iota(jnp.int32, (16, nz), 0)

    def plane_sum(f):
        count = f.shape[0]
        flat = f.reshape(count * 16, nz)
        after = pltpu.roll(flat, nz - 1, 1).reshape(count, 16, nz)
        before = pltpu.roll(flat, 1, 1).reshape(count, 16, nz)
        f = f + jnp.where(lanes == 7, after, jnp.where(lanes == 0, before, 0.0))
        lo, hi = f[:, :8], f[:, 8:]
        new_lo = lo + jnp.where(row == 7, pltpu.roll(hi, 7, 1), 0.0)
        new_hi = hi + jnp.where(row == 0, pltpu.roll(lo, 1, 1), 0.0)
        return jnp.concatenate([new_lo, new_hi], axis=1)

    def local_sum(f):
        f = plane_sum(f)
        shared = f[7:8] + f[8:9]
        return jnp.concatenate([f[:7], shared, shared, f[9:]], axis=0)

    def face_copies(turn):
        pairs = [
            (xs.at[turn, 1], xr.at[turn, 0], right, d),
            (xs.at[turn, 0], xr.at[turn, 1], left, d),
            (ys.at[turn, 1, pl.ds(0, 16)], yr.at[turn, 0, pl.ds(0, 16)], w, up),
            (ys.at[turn, 0, pl.ds(0, 16)], yr.at[turn, 1, pl.ds(0, 16)], w, down),
            (es.at[turn, 3], er.at[turn, 0], right, up),
            (es.at[turn, 2], er.at[turn, 1], right, down),
            (es.at[turn, 1], er.at[turn, 2], left, up),
            (es.at[turn, 0], er.at[turn, 3], left, down),
        ]
        return [
            pltpu.make_async_remote_copy(
                src_ref=src,
                dst_ref=dst,
                send_sem=face_send.at[turn, index],
                recv_sem=face_recv.at[turn, index],
                device_id={"wide": to_w, "deep": to_d},
                device_id_type=MESH,
            )
            for index, (src, dst, to_w, to_d) in enumerate(pairs)
        ]

    def begin(turn, f):
        f = local_sum(f)
        xs[turn, 0] = f[0]
        xs[turn, 1] = f[15]
        ys[turn, 0, 0:16] = f[:, 0:1]
        ys[turn, 1, 0:16] = f[:, 15:16]
        es[turn, 0] = f[0, 0:1]
        es[turn, 1] = f[0, 15:16]
        es[turn, 2] = f[15, 0:1]
        es[turn, 3] = f[15, 15:16]
        copies = face_copies(turn)
        for copy in copies:
            copy.start()
        return f, copies

    def add_rows(f, low, high):
        lo = f[:, :8] + jnp.where(row == 0, low, 0.0)
        hi = f[:, 8:] + jnp.where(row == 7, high, 0.0)
        return jnp.concatenate([lo, hi], axis=1)

    def ghost_copy(index, src, dst, to):
        return pltpu.make_async_remote_copy(
            src_ref=src,
            dst_ref=dst,
            send_sem=ghost_send.at[index],
            recv_sem=ghost_recv.at[index],
            device_id={"wide": to, "deep": d},
            device_id_type=MESH,
        )

    def ghost_copies():
        result = []
        for side, (to, start, face) in enumerate(((right, 8, 15), (left, 0, 0))):
            pieces = (
                (metric_ref.at[0, pl.ds(start, 8)], gm.at[side, pl.ds(0, 8)]),
                (metric_ref.at[1, face], gm.at[side, 8]),
                (metric_ref.at[2, face], gm.at[side, 9]),
                (helm_ref.at[face], gm.at[side, 10]),
            )
            for index, (src, dst) in enumerate(pieces):
                result.append(ghost_copy(side * 5 + index, src, dst, to))
        return result

    def finish(turn, f, copies):
        for copy in copies:
            copy.wait_recv()
        f = add_rows(f, yr[turn, 0, 0:16], yr[turn, 1, 0:16])

        def face(side):
            edge_lo, edge_hi = er[turn, 2 * side], er[turn, 2 * side + 1]
            return xr[turn, side] + jnp.where(
                plane == 0, edge_lo, jnp.where(plane == 15, edge_hi, 0.0)
            )

        return jnp.concatenate(
            [f[:1] + face(0)[None], f[1:15], f[15:] + face(1)[None]], axis=0
        )

    def x_apply(u, table):
        parts = u.reshape(2, 8, 16, nz)
        nodes = [parts[:, i] for i in range(8)]
        result = []
        for m in range(8):
            total = float(table[m, 0]) * nodes[0]
            for i in range(1, 8):
                total = total + float(table[m, i]) * nodes[i]
            result.append(total)
        return jnp.stack(result, axis=1).reshape(16, 16, nz)

    def y_apply(u, which):
        parts = u.reshape(-1, 8, nz)

        def coefficient(shift):
            table = yt_ref[which, shift]
            if nz > 128:
                table = jnp.concatenate([table] * (nz // 128), axis=1)
            return table[None]

        total = coefficient(0) * parts
        for shift in range(1, 8):
            total = total + coefficient(shift) * pltpu.roll(parts, shift, 1)
        return total.reshape(u.shape)

    def z_apply(u, which):
        flat = u.reshape(-1, nz)
        result = []
        for start in range(0, nz, 128):
            high, low = halves(flat[:, start : start + 128])
            both = jnp.dot(
                jnp.concatenate([high, low], axis=1), zt_ref[which], preferred_element_type=F32
            )
            result.append(both[:, :128] + both[:, 128:])
        whole = result[0] if len(result) == 1 else jnp.concatenate(result, axis=1)
        return whole.reshape(u.shape)

    def operator(u):
        total = helm_ref[...] * u
        total = total + x_apply(metric_ref[0] * x_apply(u, deriv), deriv.T)
        total = total + y_apply(metric_ref[1] * y_apply(u, 0), 1)
        return total + z_apply(metric_ref[2] * z_apply(u, 0), 1)

    for index in (1, 0, 2, 6, 7):
        loads[index].wait()
    def begin_outside_in(turn, u):
        back = x_apply(metric_ref[0] * x_apply(u, deriv), deriv.T)

        def part(pick):
            here = pick(u)
            total = pick(helm_ref[...]) * here + pick(back)
            total = total + y_apply(pick(metric_ref[1]) * y_apply(here, 0), 1)
            total = total + z_apply(pick(metric_ref[2]) * z_apply(here, 0), 1)
            return plane_sum(pick(rhs_ref[...]) - total)

        copies = face_copies(turn)
        outer = part(lambda v: jnp.concatenate([v[:1], v[15:]], axis=0))
        for side in range(2):
            xs[turn, side] = outer[side]
            es[turn, 2 * side] = outer[side, 0:1]
            es[turn, 2 * side + 1] = outer[side, 15:16]
        for index in (0, 1, 4, 5, 6, 7):
            copies[index].start()
        inner = part(lambda v: v[1:15])
        shared = inner[6:7] + inner[7:8]
        f = jnp.concatenate(
            [outer[:1], inner[:6], shared, shared, inner[8:], outer[1:]], axis=0
        )
        ys[turn, 0, 0:16] = f[:, 0:1]
        ys[turn, 1, 0:16] = f[:, 15:16]
        for index in (2, 3):
            copies[index].start()
        return f, copies

    def ghost_face(side, u, face):
        nodes = [u[i] for i in range(8)]
        total = gm[side, 10] * nodes[face]
        for m in range(8):
            slope = float(deriv[m, 0]) * nodes[0]
            for i in range(1, 8):
                slope = slope + float(deriv[m, i]) * nodes[i]
            total = total + float(deriv[m, face]) * (gm[side, m] * slope)
        total = total + y_apply(gm[side, 8] * y_apply(nodes[face], 0), 1)
        total = total + z_apply(gm[side, 9] * z_apply(nodes[face], 0), 1)
        return lr[side] - total

    square = deriv * deriv
    diagonal = helm_ref[...] + x_apply(metric_ref[0], square.T)
    diagonal = diagonal + y_apply(metric_ref[1], 2) + z_apply(metric_ref[2], 2)

    pl.semaphore_wait(barrier, nw * (1 + len(around)) - 1)
    diagonal, diagonal_copies = begin(0, diagonal)
    summed, rhs_copies = begin(1, rhs_ref[...])

    for index in (5, 3, 4, 8, 9, 10, 11, 12):
        loads[index].wait()

    v = jnp.concatenate([values_ref[0, y] for y in range(2)], axis=0)
    spread = mm(v.T, rep_ref[...]).reshape(K, BS, BS, width)
    slot_lane = lax.broadcasted_iota(jnp.int32, (BS, width), 1) % 8
    cols = jnp.concatenate([columns_ref[0, y] for y in range(2)], axis=0).astype(F32)
    live = jnp.concatenate(
        [jnp.concatenate([live_ref[0, y : y + 1, b : b + 1] for b in range(nxb)], axis=0) for y in range(2)],
        axis=0,
    )
    slot = lax.broadcasted_iota(jnp.int32, (nb, K), 1)
    cols = jnp.where(slot < live, cols, -1.0)
    cols = jnp.dot(
        cols.T.astype(BF16), rep_ref[...].astype(BF16), preferred_element_type=F32
    ).astype(jnp.int32)
    block = lax.broadcasted_iota(jnp.int32, (nw, width), 0) // 4
    sums = [jnp.zeros((nw, width), F32) for _ in range(12)]
    for k in range(K):
        chosen = jnp.zeros((BS, width), F32)
        for i in range(BS):
            chosen = chosen + jnp.where(slot_lane == i, spread[k, i], 0.0)
        placed = mm(pick_ref[...], chosen)
        for layer in range(3):
            for y in range(2):
                hit = cols[k : k + 1] == block + (layer * nb + y * nxb)
                for par in range(2):
                    at = layer * 4 + y * 2 + par
                    sums[at] = sums[at] + jnp.where(
                        hit, placed[par * nw : (par + 1) * nw], 0.0
                    )
    for at in range(12):
        m_ref[at] = sums[at]

    vertex = lax.broadcasted_iota(jnp.int32, (32, 2 * width), 0)
    lane = lax.broadcasted_iota(jnp.int32, (32, 2 * width), 1)
    yv, xv = vertex // 8, vertex % 8
    wanted_x = lax.rem(2 * w - 1 + xv + 2 * nw, 2 * nw)
    wanted = jnp.where(yv < 2, yv * 2 * nw, width) + wanted_x
    selected = jnp.where((lane == wanted) & (yv < 3) & (xv < 5), 1.0, 0.0)
    spread_ref[...] = mm(expand_ref[...], selected)

    inverse = 1.0 / finish(0, diagonal, diagonal_copies)
    inv_ref[...] = inverse
    residual = finish(1, summed, rhs_copies)
    update = inverse * residual * (1.0 / centre)
    u = update
    f, face_two = begin_outside_in(2, u)
    ghosts = ghost_copies()
    for ghost in ghosts:
        ghost.start()
    residual = finish(2, f, face_two)
    update = (second_weight * first_weight) * update + (
        (2.0 * second_weight / half_width) * inv_ref[...]
    ) * residual
    first = u + update

    local_res = rhs_ref[...] - operator(first)
    vertices = mm(corner_ref[...], local_res.reshape(256, nz))
    shifted = mm(wz3_ref[...], vertices, True)
    group = lax.broadcasted_iota(jnp.int32, (nw, 64), 1) // 16
    packed = jnp.where(
        group == 0,
        shifted[:nw],
        jnp.where(group == 1, shifted[nw : 2 * nw], shifted[2 * nw :]),
    )
    packed = jnp.concatenate([packed, jnp.zeros((nw, 64), F32)], axis=1)
    for at in range(nw):
        qs[at] = packed[at : at + 1]
    qr[0, w] = qs[w]

    def q_copy(to, to_d, which):
        return pltpu.make_async_remote_copy(
            src_ref=qs.at[to],
            dst_ref=qr.at[which, w],
            send_sem=q_send.at[which],
            recv_sem=q_recv.at[which],
            device_id={"wide": to, "deep": to_d},
            device_id_type=MESH,
        )

    def q_start(step, carry):
        to = lax.rem(w + step, nw)
        q_copy(to, up, 1).start()

        @pl.when(step > 0)
        def _():
            q_copy(to, d, 0).start()

        return carry

    lax.fori_loop(0, nw, q_start, 0)
    ls[0] = local_res[0]
    ls[1] = local_res[15]
    faces = [ghost_copy(4, ls.at[1], lr.at[0], right), ghost_copy(9, ls.at[0], lr.at[1], left)]
    for ghost in faces:
        ghost.start()
    ghosts = ghosts + faces

    def wait_rows(ref, count, which, semaphore):
        view = ref.at[which, pl.ds(0, count)]
        pltpu.make_async_copy(view, view, semaphore).wait()

    wait_rows(qr, nw - 1, 0, q_recv.at[0])
    wait_rows(qr, nw, 1, q_recv.at[1])
    own = jnp.concatenate([qr[0, at] for at in range(nw)], axis=0)
    below = jnp.concatenate([qr[1, at] for at in range(nw)], axis=0)
    frame = own + pltpu.roll(below, 128 - 8, 1)
    frame = frame + pltpu.roll(pltpu.roll(frame, 1, 0), 128 - 2, 1)
    total = jnp.zeros((nw, width), F32)
    for layer in range(3):
        for y in range(2):
            for par in range(2):
                at = layer * 16 + y * 4 + par
                total = total + m_ref[layer * 4 + y * 2 + par] * frame[:, at : at + 1]
    product = jnp.sum(total, axis=0, keepdims=True)
    cs[0] = product
    cr[0, w] = product
    product_ref[0, 0:1] = product[:, : 2 * nw]
    product_ref[0, 1:2] = product[:, 2 * nw :]

    def c_copy(to, to_d, which):
        return pltpu.make_async_remote_copy(
            src_ref=cs.at[0],
            dst_ref=cr.at[which, w],
            send_sem=c_send.at[which],
            recv_sem=c_recv.at[which],
            device_id={"wide": to, "deep": to_d},
            device_id_type=MESH,
        )

    def c_start(step, carry):
        to = lax.rem(w + step, nw)
        c_copy(to, down, 1).start()

        @pl.when(step > 0)
        def _():
            c_copy(to, d, 0).start()

        return carry

    lax.fori_loop(0, nw, c_start, 0)
    wait_rows(cr, nw - 1, 0, c_recv.at[0])
    wait_rows(cr, nw, 1, c_recv.at[1])
    mine = jnp.concatenate([cr[0, at] for at in range(nw)], axis=0)
    above = jnp.concatenate([cr[1, at] for at in range(nw)], axis=0)
    both = jnp.concatenate([mine, above], axis=1)
    correction = mm(mm(spread_ref[...], both, True), wz3_ref[nw : 2 * nw])
    for ghost in ghosts:
        ghost.wait_recv()
    correction = correction.reshape(32, 16, nz)
    outer = jnp.stack(
        [ghost_face(0, correction[:8], 7), ghost_face(1, correction[24:], 0)], axis=0
    )
    outer = plane_sum(outer)
    correction = correction[8:24]
    u = first + correction
    f = local_sum(local_res - operator(correction))
    for side, edge in ((0, 0), (1, 15)):
        ys[3, side, 0:16] = f[:, edge : edge + 1]
        ys[3, side, 16:18] = outer[:, edge : edge + 1]
    face_three = [
        pltpu.make_async_remote_copy(
            src_ref=ys.at[3, 1 - side],
            dst_ref=yr.at[3, side],
            send_sem=face_send.at[3, side],
            recv_sem=face_recv.at[3, side],
            device_id={"wide": w, "deep": to},
            device_id_type=MESH,
        )
        for side, to in ((0, up), (1, down))
    ]
    for copy in face_three:
        copy.start()
    for copy in face_three:
        copy.wait_recv()
    outer = add_rows(outer, yr[3, 0, 16:18], yr[3, 1, 16:18])
    f = add_rows(f, yr[3, 0, 0:16], yr[3, 1, 0:16])
    f = jnp.concatenate([f[:1] + outer[:1], f[1:15], f[15:] + outer[1:]], axis=0)
    update = inv_ref[...] * f * (1.0 / centre)
    u = u + update
    f, face_four = begin_outside_in(4, u)
    residual = finish(4, f, face_four)
    update = (second_weight * first_weight) * update + (
        (2.0 * second_weight / half_width) * inv_ref[...]
    ) * residual
    out_ref[...] = u + update

    for copies in (diagonal_copies, rhs_copies, face_two, ghosts, face_three, face_four):
        for copy in copies:
            copy.wait_send()
    wait_rows(qr, nw - 1, 0, q_send.at[0])
    wait_rows(qr, nw, 1, q_send.at[1])
    wait_rows(cr, nw - 1, 0, c_send.at[0])
    wait_rows(cr, nw, 1, c_send.at[1])


def local(nw, nd, *arguments):
    rhs = arguments[0]
    nz = rhs.shape[2]
    deriv, tables = tables_of(nw, nz)
    width = 4 * nw
    vmem = pl.BlockSpec(memory_space=pltpu.VMEM)
    return pl.pallas_call(
        functools.partial(kernel, nw, nd, deriv),
        out_shape=(
            jax.ShapeDtypeStruct(rhs.shape, F32),
            jax.ShapeDtypeStruct((1, 2, 2 * nw), F32),
        ),
        in_specs=[pl.BlockSpec(memory_space=pltpu.HBM)] * 13,
        out_specs=(vmem, vmem),
        scratch_shapes=[pltpu.VMEM(a.shape, a.dtype) for a in (*arguments, *tables)]
        + [
            pltpu.VMEM((5, 2, 16, nz), F32),
            pltpu.VMEM((5, 2, 18, 1, nz), F32),
            pltpu.VMEM((5, 4, 1, nz), F32),
            pltpu.VMEM((5, 2, 16, nz), F32),
            pltpu.VMEM((5, 2, 18, 1, nz), F32),
            pltpu.VMEM((5, 4, 1, nz), F32),
            pltpu.VMEM((nw, 1, 128), F32),
            pltpu.VMEM((2, nw, 1, 128), F32),
            pltpu.VMEM((1, 1, width), F32),
            pltpu.VMEM((2, nw, 1, width), F32),
            pltpu.VMEM((2, 11, 16, nz), F32),
            pltpu.VMEM((2, 16, nz), F32),
            pltpu.VMEM((2, 16, nz), F32),
            pltpu.VMEM((16, 16, nz), F32),
            pltpu.VMEM((12, nw, width), F32),
            pltpu.VMEM((512, 2 * width), F32),
            pltpu.SemaphoreType.DMA((5, 8)),
            pltpu.SemaphoreType.DMA((5, 8)),
            pltpu.SemaphoreType.DMA((2,)),
            pltpu.SemaphoreType.DMA((2,)),
            pltpu.SemaphoreType.DMA((2,)),
            pltpu.SemaphoreType.DMA((2,)),
            pltpu.SemaphoreType.DMA((10,)),
            pltpu.SemaphoreType.DMA((10,)),
            pltpu.SemaphoreType.DMA((13,)),
        ],
        compiler_params=pltpu.CompilerParams(
            collective_id=0, has_side_effects=True, vmem_limit_bytes=63 * 1024 * 1024
        ),
    )(*arguments, *tables)


def solution(mesh):
    placed = (
        P("wide", "deep", None),
        P(None, "wide", "deep", None),
        P("wide", "deep", None),
        P("wide", "deep", None, None),
        P("wide", "deep", None),
        P("wide", "deep", None, None),
    )
    return jax.shard_map(
        functools.partial(local, mesh.shape["wide"], mesh.shape["deep"]),
        mesh=mesh,
        in_specs=placed,
        out_specs=(P("wide", "deep", None), P("wide", "deep", None)),
        check_vma=False,
    )
```
